128 devices in a mesh: row: 8 (over y, core), col: 16 (over x, z).
Axes of the slice: x: 4, y: 4, z: 4, core: 2. Of those that a mesh axis runs over, the one named last changes fastest.
Arguments:
- kernel: float32 [2, 8, 1, 16, 640, 640], P(None, 'row', None, 'col'), as said below
Outputs:
- factored: float32 [2, 8, 1, 16, 640, 640], P(None, 'row', None, 'col')
Inputs may be any that keep to these rules, and one draw needn't show every extreme that they name: kernel is the tile layout of a symmetric positive definite matrix.
All inputs are finite; a program needn't handle non-finite values.
Results may differ from the reference program's by a relative error of at most 0.00011.
Values sent between devices are 32-bit elements; how exact they have to be, the bound alone decides.
No kernel may reach another device: no remote copies, remote signals or barrier semaphores. Data moves between devices by JAX's collectives and lax.ppermute only.
A program may use at most 128 MiB of HBM per device.

```python
import jax
import jax.numpy as jnp
from jax import lax

TILE = 640
TC_DEV = 1
TR_DEV = 2
ORDER = 10240
N_ROW = 8
N_COL = 16


def draw_kernel(key, part):
    key = jax.random.fold_in(key, 7)
    key_first, key_second, key_scale, key_diag = jax.random.split(key, 4)
    coord_one = jax.random.uniform(key_first, (ORDER,), jnp.float32, 0.0, 1.0)
    coord_two = jax.random.uniform(key_second, (ORDER,), jnp.float32, 0.0, 1.0)
    spread = 0.5
    diag_lift = jax.random.uniform(key_diag, (ORDER,), jnp.float32, 1.0, 3.0)
    scales = jnp.exp(jax.random.uniform(key_scale, (ORDER,), jnp.float32, -spread, spread))
    distance = jnp.abs(coord_one[:, None] - coord_one[None, :]) + jnp.abs(coord_two[:, None] - coord_two[None, :])
    places = jnp.arange(ORDER)
    full = scales[:, None] * scales[None, :] * jnp.exp(distance * (-1.0 / 0.08))
    full = full + jnp.where(places[:, None] == places[None, :], diag_lift[None, :], 0.0)
    tiles = full.reshape(TR_DEV, N_ROW, TILE, TC_DEV, N_COL, TILE)
    return jnp.transpose(tiles, (0, 1, 3, 4, 2, 5))


def setup_inputs(seed: int = 0) -> dict:
    arg_keys = jax.random.split(jax.random.key(seed), 2)
    kernel = draw_kernel(jax.random.fold_in(arg_keys[1], 71), 0)
    return {"kernel": kernel}


def to_full(tiles):
    return jnp.transpose(tiles, (0, 1, 4, 2, 3, 5)).reshape(ORDER, ORDER)

def to_tiles(full):
    return jnp.transpose(full.reshape(TR_DEV, N_ROW, TILE, TC_DEV, N_COL, TILE), (0, 1, 3, 4, 2, 5))

def reference(kernel):
    full = to_full(kernel)
    for step in range(2):
        start = step * TILE
        end = start + TILE
        corner = jnp.linalg.cholesky(full[start:end, start:end])
        below = full[end:, start:end]
        solved = jax.scipy.linalg.solve_triangular(corner, below.T, lower=True).T
        trailing = full[end:, end:] - jnp.dot(solved, solved.T, precision=lax.Precision.HIGHEST)
        full = full.at[start:end, start:end].set(corner)
        full = full.at[end:, start:end].set(solved)
        full = full.at[end:, end:].set(trailing)
    return to_tiles(full)
```

```python
import functools

import jax
import jax.numpy as jnp
from jax import lax
from jax.experimental import pallas as pl
from jax.experimental.pallas import tpu as pltpu
from jax.sharding import PartitionSpec as P

f32 = jnp.float32
bf16 = jnp.bfloat16
T = 640
B = 128
NB = T // B
SG = 32
HIGHEST = lax.Precision.HIGHEST
NT = (((1,), (1,)), ((), ()))
TN = (((0,), (0,)), ((), ()))


def split3(x):
    high = x.astype(bf16)
    rest = x - high.astype(f32)
    mid = rest.astype(bf16)
    low = (rest - mid.astype(f32)).astype(bf16)
    return high, mid, low


def left6(parts, axis):
    h, m, l = parts
    return jnp.concatenate([h, h, m, m, h, l], axis)


def right6(parts):
    h, m, l = parts
    return jnp.concatenate([h, m, h, m, l, h], 0)


def dot6(left, right):
    return jnp.dot(left, right, preferred_element_type=f32)


def row_of(x, m):
    return jnp.broadcast_to(x[m : m + 1, :], x.shape)


def factor_block(block):
    groups = SG // 8
    row = lax.broadcasted_iota(jnp.int32, (B, B), 0)
    col = lax.broadcasted_iota(jnp.int32, (B, B), 1)
    unit = jnp.where(row == col, 1.0, 0.0)
    sub = lax.broadcasted_iota(jnp.int32, (8, B), 0)
    count = B // SG
    work = [
        jnp.concatenate([block[s * SG : (s + 1) * SG], unit[s * SG : (s + 1) * SG]], 1)
        for s in range(count)
    ]
    uppers, inverses = [], []
    for s in range(count):
        u = [work[s][8 * h : 8 * h + 8, :B] for h in range(groups)]
        w = [work[s][8 * h : 8 * h + 8, B:] for h in range(groups)]
        for g in range(groups):
            base = s * SG + 8 * g
            c = [
                [jnp.broadcast_to(u[h][:, base + m : base + m + 1], (8, B)) for m in range(8)]
                if h >= g
                else None
                for h in range(groups)
            ]
            scale = jnp.zeros((8, B), f32)
            for m in range(8):
                pivot = row_of(c[g][m], m)
                inverse = 1.0 / pivot
                scale = jnp.where(sub == m, lax.rsqrt(pivot), scale)
                u_row = row_of(u[g], m) * inverse
                w_row = row_of(w[g], m) * inverse
                c_row = [row_of(c[g][k], m) * inverse if k > m else None for k in range(8)]
                for h in range(g, groups):
                    factor = c[h][m]
                    if h == g:
                        factor = jnp.where(sub > m, factor, 0.0)
                    for k in range(m + 1, 8):
                        c[h][k] = c[h][k] - factor * c_row[k]
                    u[h] = u[h] - factor * u_row
                    w[h] = w[h] - factor * w_row
            u[g] = u[g] * scale
            w[g] = w[g] * scale
        upper = jnp.concatenate(u, 0)
        inverse = jnp.concatenate(w, 0)
        here = lax.broadcasted_iota(jnp.int32, (SG, B), 0) + s * SG
        upper = jnp.where(lax.broadcasted_iota(jnp.int32, (SG, B), 1) >= here, upper, 0.0)
        uppers.append(upper)
        inverses.append(inverse)
        if s < count - 1:
            left = left6(split3(upper[:, (s + 1) * SG :]), 0)
            right = right6(split3(jnp.concatenate([upper, inverse], 1)))
            change = lax.dot_general(left, right, TN, preferred_element_type=f32)
            for t in range(s + 1, count):
                work[t] = work[t] - change[(t - s - 1) * SG : (t - s) * SG]
    return jnp.concatenate(uppers, 0), jnp.concatenate(inverses, 0)


def factor_tile(read, lower_ref, inverse_ref):
    panel = [read(i) for i in range(NB)]
    aug = [None] * NB
    for i in range(NB):
        for j in range(i + 1, NB):
            lower_ref[i * B : (i + 1) * B, j * B : (j + 1) * B] = jnp.zeros((B, B), f32)
            inverse_ref[i * B : (i + 1) * B, j * B : (j + 1) * B] = jnp.zeros((B, B), f32)
    for b in range(NB):
        upper, inv = factor_block(panel[b][:, :B])
        rows = slice(b * B, (b + 1) * B)
        lower_ref[rows, rows] = upper.T
        inverse_ref[rows, rows] = inv
        left = left6(split3(inv), 1)
        if b > 0:
            w_left = dot6(left, right6(split3(aug[b])))
            inverse_ref[rows, : b * B] = w_left
            w_all = jnp.concatenate([w_left, inv], 1)
        else:
            w_all = inv
        if b == NB - 1:
            break
        w_parts = right6(split3(w_all))
        pieces = [
            dot6(left, right6(split3(panel[b][:, (i - b) * B : (i - b + 1) * B])))
            for i in range(b + 1, NB)
        ]
        u_parts = right6(split3(jnp.concatenate(pieces, 1)))
        for i in range(b + 1, NB):
            off = (i - b) * B
            turned = pieces[i - b - 1].T
            lower_ref[i * B : (i + 1) * B, rows] = turned
            left_i = left6(split3(turned), 1)
            panel[i] = panel[i] - dot6(left_i, u_parts[:, off - B :])
            grown = -dot6(left_i, w_parts)
            if b > 0:
                grown = jnp.concatenate([aug[i] + grown[:, : b * B], grown[:, b * B :]], 1)
            aug[i] = grown


def at_root():
    return (lax.axis_index("row") == 0) & (lax.axis_index("col") == 0)


def first_kernel(tiles_ref, lower_ref, inverse_ref, sem):
    @pl.when(at_root())
    def _():
        copy = pltpu.make_async_copy(tiles_ref.at[0], lower_ref, sem)
        copy.start()
        copy.wait()
        blocks = [lower_ref[i * B : (i + 1) * B, i * B :] for i in range(NB)]
        factor_tile(lambda i: blocks[i], lower_ref, inverse_ref)


def product(left_ref, right_ref, out_ref, dims, base=None, sign=1.0):
    def step(i, carry):
        rows = pl.ds(pl.multiple_of(i * B, B), B)
        if dims is TN:
            left = left_ref[:, rows]
        else:
            left = left_ref[rows, :]
        got = lax.dot_general(left, right_ref[...], dims, precision=HIGHEST, preferred_element_type=f32)
        if base is not None:
            got = base[rows, :] + got if sign > 0 else base[rows, :] - got
        out_ref[rows, :] = got
        return carry

    lax.fori_loop(0, NB, step, 0)


NN = (((1,), (0,)), ((), ()))


def second_kernel(left_ref, corner_ref, inverse_ref, panel_ref, lower_ref, inverse2_ref, scratch):
    @pl.when(at_root())
    def _():
        product(left_ref, inverse_ref, panel_ref, NT)
        product(panel_ref, panel_ref, scratch, NT, corner_ref, -1.0)
        factor_tile(lambda i: scratch[i * B : (i + 1) * B, i * B :], lower_ref, inverse2_ref)


def last_kernel(tiles_ref, row_ref, col_ref, first_ref, w0_ref, panel_ref, w1_ref, out_ref,
                y0c, y1c, y0, y1, temp):
    r = lax.axis_index("row")
    c = lax.axis_index("col")

    def solve(top, bottom, top_out, bottom_out):
        product(w0_ref, top, top_out, NN)
        product(panel_ref, top_out, temp, NN, bottom, -1.0)
        product(w1_ref, temp, bottom_out, NN)

    @pl.when(c > 1)
    def _():
        solve(col_ref.at[pl.ds(0, T)], col_ref.at[pl.ds(T, T)], y0c, y1c)

    for a in range(2):
        tile = tiles_ref.at[a]
        out = out_ref.at[a]
        solve(row_ref.at[pl.ds(2 * a * T, T)], row_ref.at[pl.ds((2 * a + 1) * T, T)], y0, y1)
        top = r if a == 0 else r + 8

        @pl.when((c > 1) & (top > 0))
        def _():
            product(y0, y0c, out, TN, tile, -1.0)

        @pl.when((c > 1) & (top > 1))
        def _():
            product(y1, y1c, out, TN, out, -1.0)

        @pl.when((top == 0) & (c > 0))
        def _():
            out[...] = tile[...]

        @pl.when((top == 0) & (c == 0))
        def _():
            out[...] = first_ref[...]

        @pl.when((top > 0) & (c == 0))
        def _():
            out[...] = y0[...].T

        @pl.when((top > 0) & (c == 1))
        def _():
            turned = y1[...].T
            row = lax.broadcasted_iota(jnp.int32, (T, T), 0)
            col = lax.broadcasted_iota(jnp.int32, (T, T), 1)
            out[...] = jnp.where((top == 1) & (col > row), 0.0, turned)


VMEM = pl.BlockSpec(memory_space=pltpu.VMEM)
ANY = pl.BlockSpec(memory_space=pl.ANY)
PARAMS = pltpu.CompilerParams(vmem_limit_bytes=56 << 20)
TILE = jax.ShapeDtypeStruct((T, T), f32)


def place(x, y, z, core):
    return (y * 2 + core) * 16 + x * 4 + z


def tree():
    every = range(4)
    root = place(0, 0, 0, 0)
    levels = [[(root, place(1, 0, 0, 0))]]
    levels.append([(root, place(3, 0, 0, 0)), (place(1, 0, 0, 0), place(2, 0, 0, 0))])
    levels.append([(place(x, 0, 0, 0), place(x, 0, 1, 0)) for x in every])
    levels.append(
        [(place(x, 0, 0, 0), place(x, 0, 3, 0)) for x in every]
        + [(place(x, 0, 1, 0), place(x, 0, 2, 0)) for x in every]
    )
    levels.append([(place(x, 0, z, 0), place(x, 1, z, 0)) for x in every for z in every])
    levels.append(
        [(place(x, 0, z, 0), place(x, 3, z, 0)) for x in every for z in every]
        + [(place(x, 1, z, 0), place(x, 2, z, 0)) for x in every for z in every]
    )
    levels.append(
        [(place(x, y, z, 0), place(x, y, z, 1)) for x in every for y in every for z in every]
    )
    return levels


def spread(piece):
    piece = jnp.where(at_root(), piece, 0.0)
    for pairs in tree():
        piece = piece + lax.ppermute(piece, ("row", "col"), pairs)
    return piece


def spread_tile(tile, low):
    if low:
        one = spread(tile[: 3 * B, : 3 * B])
        two = spread(tile[3 * B :])
        return jnp.concatenate([jnp.pad(one, ((0, 0), (0, 2 * B))), two], 0)
    return jnp.concatenate([spread(tile[: 2 * B]), spread(tile[2 * B : 4 * B]), spread(tile[4 * B :])], 0)


def gather_rows(top):
    flat = top.reshape(4, T // 4, T)
    shard = None
    for m in range(4):
        pairs = [
            (h * 16 + j, (j % 8) * 16 + (j // 8) * 8 + h * 4 + m)
            for j in range(1, 16)
            for h in range(2)
        ]
        got = lax.ppermute(flat[m], ("row", "col"), pairs)
        shard = got if shard is None else shard + got
    return lax.all_gather(shard, "col", axis=0, tiled=True)


def gather_cols(top):
    flat = top.reshape(4, T // 4, T)
    shard = None
    for m in range(4):
        pairs = [(h * 16 + c, (h * 4 + m) * 16 + c) for c in range(1, 16) for h in range(2)]
        got = lax.ppermute(flat[m], ("row", "col"), pairs)
        shard = got if shard is None else shard + got
    return lax.all_gather(shard, "row", axis=0, tiled=True)


def shards(kernel):
    tiles = kernel.reshape(2, T, T)
    left = lax.ppermute(tiles[0], ("row", "col"), [(16, 0)])
    corner = lax.ppermute(tiles[0], ("row", "col"), [(17, 0)])
    rows = gather_rows(tiles[0])
    cols = gather_cols(tiles[0])
    first, w0 = pl.pallas_call(
        first_kernel,
        out_shape=[TILE, TILE],
        in_specs=[ANY],
        out_specs=[VMEM, VMEM],
        scratch_shapes=[pltpu.SemaphoreType.DMA],
        compiler_params=PARAMS,
        name="factor_first",
    )(tiles)
    panel, _, w1 = pl.pallas_call(
        second_kernel,
        out_shape=[TILE, TILE, TILE],
        in_specs=[VMEM] * 3,
        out_specs=[VMEM] * 3,
        scratch_shapes=[pltpu.VMEM((T, T), f32)],
        compiler_params=PARAMS,
        name="factor_second",
    )(left, corner, w0)
    w0 = spread_tile(w0, True)
    panel = spread_tile(panel, False)
    w1 = spread_tile(w1, True)
    out = pl.pallas_call(
        last_kernel,
        out_shape=jax.ShapeDtypeStruct((2, T, T), f32),
        in_specs=[VMEM] * 7,
        out_specs=VMEM,
        scratch_shapes=[pltpu.VMEM((T, T), f32)] * 5,
        compiler_params=PARAMS,
        name="solve_and_update",
    )(tiles, rows, cols, first, w0, panel, w1)
    return out.reshape(kernel.shape)


def solution(mesh):
    spec = P(None, "row", None, "col", None, None)
    return jax.shard_map(shards, mesh=mesh, in_specs=(spec,), out_specs=spec, check_vma=False)
```

```python
import functools

import jax
import jax.numpy as jnp
from jax import lax
from jax.experimental import pallas as pl
from jax.experimental.pallas import tpu as pltpu
from jax.sharding import PartitionSpec as P

f32 = jnp.float32
bf16 = jnp.bfloat16
T = 640
B = 128
NB = T // B
SG = 32
HIGHEST = lax.Precision.HIGHEST
NT = (((1,), (1,)), ((), ()))
TN = (((0,), (0,)), ((), ()))


def split3(x):
    high = x.astype(bf16)
    rest = x - high.astype(f32)
    mid = rest.astype(bf16)
    low = (rest - mid.astype(f32)).astype(bf16)
    return high, mid, low


def left6(parts, axis):
    h, m, l = parts
    return jnp.concatenate([h, h, m, m, h, l], axis)


def right6(parts):
    h, m, l = parts
    return jnp.concatenate([h, m, h, m, l, h], 0)


def dot6(left, right):
    return jnp.dot(left, right, preferred_element_type=f32)


def row_of(x, m):
    return jnp.broadcast_to(x[m : m + 1, :], x.shape)


def factor_block(block):
    groups = SG // 8
    row = lax.broadcasted_iota(jnp.int32, (B, B), 0)
    col = lax.broadcasted_iota(jnp.int32, (B, B), 1)
    unit = jnp.where(row == col, 1.0, 0.0)
    sub = lax.broadcasted_iota(jnp.int32, (8, B), 0)
    count = B // SG
    work = [
        jnp.concatenate([block[s * SG : (s + 1) * SG], unit[s * SG : (s + 1) * SG]], 1)
        for s in range(count)
    ]
    uppers, inverses = [], []
    for s in range(count):
        u = [work[s][8 * h : 8 * h + 8, :B] for h in range(groups)]
        w = [work[s][8 * h : 8 * h + 8, B:] for h in range(groups)]
        for g in range(groups):
            base = s * SG + 8 * g
            c = [
                [jnp.broadcast_to(u[h][:, base + m : base + m + 1], (8, B)) for m in range(8)]
                if h >= g
                else None
                for h in range(groups)
            ]
            scale = jnp.zeros((8, B), f32)
            for m in range(8):
                pivot = row_of(c[g][m], m)
                inverse = pltpu.reciprocal(pivot)
                scale = jnp.where(sub == m, lax.rsqrt(pivot), scale)
                u_row = row_of(u[g], m) * inverse
                w_row = row_of(w[g], m) * inverse
                c_row = [row_of(c[g][k], m) * inverse if k > m else None for k in range(8)]
                for h in range(g, groups):
                    factor = c[h][m]
                    if h == g:
                        factor = jnp.where(sub > m, factor, 0.0)
                    for k in range(m + 1, 8):
                        c[h][k] = c[h][k] - factor * c_row[k]
                    u[h] = u[h] - factor * u_row
                    w[h] = w[h] - factor * w_row
            u[g] = u[g] * scale
            w[g] = w[g] * scale
        upper = jnp.concatenate(u, 0)
        inverse = jnp.concatenate(w, 0)
        here = lax.broadcasted_iota(jnp.int32, (SG, B), 0) + s * SG
        upper = jnp.where(lax.broadcasted_iota(jnp.int32, (SG, B), 1) >= here, upper, 0.0)
        uppers.append(upper)
        inverses.append(inverse)
        if s < count - 1:
            left = left6(split3(upper[:, (s + 1) * SG :]), 0)
            right = right6(split3(jnp.concatenate([upper, inverse], 1)))
            change = lax.dot_general(left, right, TN, preferred_element_type=f32)
            for t in range(s + 1, count):
                work[t] = work[t] - change[(t - s - 1) * SG : (t - s) * SG]
    return jnp.concatenate(uppers, 0), jnp.concatenate(inverses, 0)


def factor_tile(read, lower_ref, inverse_ref):
    panel = [read(i) for i in range(NB)]
    aug = [None] * NB
    for i in range(NB):
        for j in range(i + 1, NB):
            lower_ref[i * B : (i + 1) * B, j * B : (j + 1) * B] = jnp.zeros((B, B), f32)
            inverse_ref[i * B : (i + 1) * B, j * B : (j + 1) * B] = jnp.zeros((B, B), f32)
    for b in range(NB):
        upper, inv = factor_block(panel[b][:, :B])
        rows = slice(b * B, (b + 1) * B)
        lower_ref[rows, rows] = upper.T
        inverse_ref[rows, rows] = inv
        left = left6(split3(inv), 1)
        if b > 0:
            w_left = dot6(left, right6(split3(aug[b])))
            inverse_ref[rows, : b * B] = w_left
            w_all = jnp.concatenate([w_left, inv], 1)
        else:
            w_all = inv
        if b == NB - 1:
            break
        w_parts = right6(split3(w_all))
        pieces = [
            dot6(left, right6(split3(panel[b][:, (i - b) * B : (i - b + 1) * B])))
            for i in range(b + 1, NB)
        ]
        u_parts = right6(split3(jnp.concatenate(pieces, 1)))
        for i in range(b + 1, NB):
            off = (i - b) * B
            turned = pieces[i - b - 1].T
            lower_ref[i * B : (i + 1) * B, rows] = turned
            left_i = left6(split3(turned), 1)
            panel[i] = panel[i] - dot6(left_i, u_parts[:, off - B :])
            grown = -dot6(left_i, w_parts)
            if b > 0:
                grown = jnp.concatenate([aug[i] + grown[:, : b * B], grown[:, b * B :]], 1)
            aug[i] = grown


def at_root():
    return (lax.axis_index("row") == 0) & (lax.axis_index("col") == 0)


def first_kernel(tiles_ref, lower_ref, inverse_ref, sem):
    @pl.when(at_root())
    def _():
        copy = pltpu.make_async_copy(tiles_ref.at[0], lower_ref, sem)
        copy.start()
        copy.wait()
        blocks = [lower_ref[i * B : (i + 1) * B, i * B :] for i in range(NB)]
        factor_tile(lambda i: blocks[i], lower_ref, inverse_ref)


def split2(x):
    high = x.astype(bf16)
    return high, (x - high.astype(f32)).astype(bf16)


def keep_parts(ref, parts):
    def step(i, carry):
        rows = pl.ds(pl.multiple_of(i * B, B), B)
        for n, part in enumerate(split3(ref[rows, :])):
            parts[rows, n * T : (n + 1) * T] = part
        return carry

    lax.fori_loop(0, NB, step, 0)


def stacked(parts, order, rows, depth):
    return jnp.concatenate([parts[rows, n * T : n * T + depth] for n in order], 1)


LEFT = (0, 0, 1, 1, 0, 2)
RIGHT = (0, 1, 0, 1, 2, 0)
GROUPS = ((0, 256, 256), (256, 256, 512), (512, 128, 640))


def times_inverse(tile_ref, inverse_ref, out_ref, tile_parts, inverse_parts):
    keep_parts(tile_ref, tile_parts)
    keep_parts(inverse_ref, inverse_parts)
    for first, count, depth in GROUPS:
        rows = slice(first, first + count)
        left = stacked(tile_parts, LEFT, slice(None), depth)
        right = stacked(inverse_parts, RIGHT, rows, depth)
        out_ref[:, rows] = lax.dot_general(left, right, NT, preferred_element_type=f32)


def second_kernel(left_ref, corner_ref, inverse_ref, out_ref, panel, lower, parts, more):
    @pl.when(at_root())
    def _():
        times_inverse(left_ref, inverse_ref, panel, parts, more)
        keep_parts(panel, parts)
        for i in range(NB):
            left = stacked(parts, LEFT, slice(i * B, (i + 1) * B), T)
            right = stacked(parts, RIGHT, slice(i * B, T), T)
            change = lax.dot_general(left, right, NT, preferred_element_type=f32)
            lower[i * B : (i + 1) * B, i * B :] = corner_ref[i * B : (i + 1) * B, i * B :] - change
        blocks = [lower[i * B : (i + 1) * B, i * B :] for i in range(NB)]
        factor_tile(lambda i: blocks[i], lower, out_ref)


def panel_kernel(tiles_ref, inverse_ref, out_ref, tile, parts, more, sem):
    @pl.when((lax.axis_index("row") == 1) & (lax.axis_index("col") == 0))
    def _():
        copy = pltpu.make_async_copy(tiles_ref.at[0], tile, sem)
        copy.start()
        copy.wait()
        times_inverse(tile, inverse_ref, out_ref, parts, more)


CHUNKS = ((0, 512), (512, 512), (1024, 512), (1536, 384))
W_PIECES = ((0, 192, 384), (192, 192, 384), (384, 128, 640), (512, 128, 640))
L_PIECES = ((0, 160, 640), (160, 160, 640), (320, 160, 640), (480, 160, 640))


def triangular(w_ref, parts, xh, xl, emit):
    high, low = split2(w_ref[...])
    parts[0] = high
    parts[1] = low
    for n, width in CHUNKS:
        for first, count, depth in GROUPS:
            wh = parts[0, first : first + count, :depth]
            wl = parts[1, first : first + count, :depth]
            top = xh[:depth, n : n + width]
            both = dot6(jnp.concatenate([wh, wl], 0), top)
            rest = dot6(wh, xl[:depth, n : n + width])
            emit(first, count, n, width, both[:count] + both[count:] + rest)


def last_kernel(*refs):
    tiles_ref, rows_ref, cols_ref, first_ref, own_ref, got_ref = refs[:6]
    moved = refs[6:18]
    out_ref = refs[18]
    x0, x1, wa, la, wb, tile, xh, xl, yh, yl, yf, parts, lparts, sems = refs[19:]
    r = lax.axis_index("row")
    c = lax.axis_index("col")
    odd = lax.rem(r, 2) == 1
    inner = c > 0
    used = iter(range(40))

    def copy(src, dst, sem=None):
        return pltpu.make_async_copy(src, dst, sems.at[next(used) if sem is None else sem])

    first_x = [
        copy(rows_ref.at[pl.ds(0, T)], x0.at[:, pl.ds(0, T)]),
        copy(rows_ref.at[pl.ds(2 * T, T)], x0.at[:, pl.ds(T, T)]),
        copy(cols_ref.at[pl.ds(0, T)], x0.at[:, pl.ds(2 * T, T)]),
    ]
    second_x = [
        copy(rows_ref.at[pl.ds(T, T)], x1.at[:, pl.ds(0, T)]),
        copy(rows_ref.at[pl.ds(3 * T, T)], x1.at[:, pl.ds(T, T)]),
        copy(cols_ref.at[pl.ds(T, T)], x1.at[:, pl.ds(2 * T, T)]),
    ]
    old = [copy(tiles_ref.at[a], tile.at[a]) for a in range(2)]
    new = [copy(tile.at[a], out_ref.at[a]) for a in range(2)]
    whole_sem = next(used)
    own = copy(own_ref, wa, whole_sem)
    got = copy(got_ref, wa, whole_sem)
    lower = copy(first_ref, tile.at[0], next(used))

    def pieces(cur, swap, dst, spec):
        places = [dst.at[pl.ds(a, n), pl.ds(0, w)] for a, n, w in spec]
        ids = [next(used), next(used)]
        here = [copy(swap, places[0], ids[0]), copy(cur, places[1], ids[1])]
        there = [copy(cur, places[0], ids[0]), copy(swap, places[1], ids[1])]
        return here, there

    w0_pairs = [pieces(moved[2 * k], moved[2 * k + 1], wa, W_PIECES[2 * k : 2 * k + 2]) for k in range(2)]
    l_pairs = [pieces(moved[4 + 2 * k], moved[5 + 2 * k], la, L_PIECES[2 * k : 2 * k + 2]) for k in range(2)]
    w1_pairs = [pieces(moved[8 + 2 * k], moved[9 + 2 * k], wb, W_PIECES[2 * k : 2 * k + 2]) for k in range(2)]

    def start(pairs):
        @pl.when(odd)
        def _():
            for _, there in pairs:
                for one in there:
                    one.start()

        @pl.when(jnp.logical_not(odd))
        def _():
            for here, _ in pairs:
                for one in here:
                    one.start()

    def wait(pairs):
        for here, _ in pairs:
            for one in here:
                one.wait()

    for one in first_x:
        one.start()

    @pl.when((c == 0) & (r == 0))
    def _():
        own.start()

    @pl.when((c == 0) & (r == 1))
    def _():
        got.start()

    @pl.when((c > 0) | (r > 1))
    def _():
        wa[: 3 * B, 3 * B :] = jnp.zeros((3 * B, 2 * B), f32)
        start(w0_pairs)

    @pl.when(inner)
    def _():
        for one in second_x:
            one.start()
        start(l_pairs)
        wb[: 3 * B, 3 * B :] = jnp.zeros((3 * B, 2 * B), f32)
        start(w1_pairs)
        for one in old:
            one.start()

    for one in first_x:
        one.wait()

    def cut(i, carry):
        rows = pl.ds(pl.multiple_of(i * B, B), B)
        xh[rows, :], xl[rows, :] = split2(x0[rows, :])
        return carry

    lax.fori_loop(0, NB, cut, 0)

    @pl.when((c == 0) & (r < 2))
    def _():
        own.wait()

    @pl.when((c > 0) | (r > 1))
    def _():
        wait(w0_pairs)

    def emit(base):
        def store(first, count, n, width, y):
            rows = slice(base + first, base + first + count)
            yh[rows, n : n + width], yl[rows, n : n + width] = split2(y)
            keep = min(width, 2 * T - n)
            if keep > 0:
                yf[first : first + count, n : n + keep] = y[:, :keep]

        return store

    triangular(wa, parts, xh, xl, emit(0))

    @pl.when(inner)
    def _():
        for one in second_x:
            one.wait()
        wait(l_pairs)
        lparts[:, :T], lparts[:, T:] = split2(la[...])

        def step(i, carry):
            at = pl.ds(pl.multiple_of(i * T, B), T)
            left = jnp.concatenate([lparts[:, :T], lparts[:, :T], lparts[:, T:]], 1)
            high = yh[:T, at]
            right = jnp.concatenate([high, yl[:T, at], high], 0)
            xh[:, at], xl[:, at] = split2(x1[:, at] - dot6(left, right))
            return carry

        lax.fori_loop(0, 3, step, 0)
        wait(w1_pairs)
        triangular(wb, parts, xh, xl, emit(T))
        for one in old:
            one.wait()

    @pl.when(r == 1)
    def _():
        yh[T:, :T] = jnp.zeros((T, T), bf16)
        yl[T:, :T] = jnp.zeros((T, T), bf16)

    for a in range(2):
        top = r + 8 * a

        @pl.when((c > 1) & (top > 0))
        def _():
            def step(i, carry):
                at = pl.ds(pl.multiple_of(a * T + i * B, B), B)
                rows = pl.ds(pl.multiple_of(i * B, B), B)
                high = yh[:, at]
                left = jnp.concatenate([high, yl[:, at]], 1)
                both = lax.dot_general(left, yh[:, 2 * T :], TN, preferred_element_type=f32)
                rest = lax.dot_general(high, yl[:, 2 * T :], TN, preferred_element_type=f32)
                tile[a, rows, :] = tile[a, rows, :] - (both[:B] + both[B:] + rest)
                return carry

            lax.fori_loop(0, NB, step, 0)

        @pl.when((top == 0) & (c == 0))
        def _():
            lower.start()
            lower.wait()

        @pl.when((top > 0) & (c < 2))
        def _():
            turned = yf[:, a * T : (a + 1) * T].T
            row = lax.broadcasted_iota(jnp.int32, (T, T), 0)
            col = lax.broadcasted_iota(jnp.int32, (T, T), 1)
            tile[a] = jnp.where((top == 1) & (c == 1) & (col > row), 0.0, turned)

        new[a].start()
    for one in new:
        one.wait()


VMEM = pl.BlockSpec(memory_space=pltpu.VMEM)
ANY = pl.BlockSpec(memory_space=pl.ANY)
PARAMS = pltpu.CompilerParams(vmem_limit_bytes=56 << 20)
TILE = jax.ShapeDtypeStruct((T, T), f32)
PARTS = pltpu.VMEM((T, 3 * T), bf16)
GRID = ("row", "col")


def place(x, y, z, core):
    return (y * 2 + core) * 16 + x * 4 + z


def tree(core, away):
    every = range(4)
    z0, z1, z2, z3 = (1, 2, 0, 3) if away else (0, 1, 3, 2)
    at = functools.partial(place, core=core)
    rounds = [
        [(at(0, 0, z0), at(1, 0, z0))],
        [(at(0, 0, z0), at(3, 0, z0)), (at(1, 0, z0), at(2, 0, z0))],
        [(at(x, 0, z0), at(x, 0, z1)) for x in every],
        [(at(x, 0, z0), at(x, 0, z2)) for x in every if x or not away]
        + [(at(x, 0, z1), at(x, 0, z3)) for x in every],
    ]
    spots = [(x, z) for x in every for z in every if x or z or not away]
    rounds.append([(at(x, 0, z), at(x, 1, z)) for x, z in spots])
    rounds.append(
        [(at(x, 0, z), at(x, 3, z)) for x, z in spots] + [(at(x, 1, z), at(x, 2, z)) for x, z in spots]
    )
    return rounds


def grow(cur, away):
    for one, two in zip(tree(1, False), tree(0, away)):
        cur = cur + lax.ppermute(cur, GRID, one + two)
    if away:
        pairs = [(place(0, y, 1, 0), place(0, y, 0, 0)) for y in range(1, 4)]
        cur = cur + lax.ppermute(cur, GRID, pairs)
    chips = [(x, y, z) for x in range(4) for y in range(4) for z in range(4)]
    if away:
        chips = chips[1:]
    pairs = [(place(*chip, k), place(*chip, 1 - k)) for chip in chips for k in range(2)]
    return cur, lax.ppermute(cur, GRID, pairs)


def spread_early(one, two, me):
    got = lax.ppermute(two, GRID, [(16, 1)])
    return grow(jnp.where(me == 16, one, got), True)


def spread_late(got, two, me):
    return grow(jnp.where(me == 0, two, got), False)


def cut_out(tile, spec):
    return [tile[a : a + n, :w] for a, n, w in spec]


def scatter_rows(tiles):
    flat = tiles[0].reshape(4, T // 4, T)
    shard = None
    for m in range(4):
        pairs = [
            (h * 16 + j, (j % 8) * 16 + (j // 8) * 8 + h * 4 + m)
            for j in range(1, 16)
            for h in range(2)
        ]
        got = lax.ppermute(flat[m], GRID, pairs)
        shard = got if shard is None else shard + got
    return shard


def scatter_cols(tiles):
    flat = tiles[0].reshape(4, T // 4, T)
    shard = None
    for m in range(4):
        pairs = [(h * 16 + c, (h * 4 + m) * 16 + c) for c in range(1, 16) for h in range(2)]
        got = lax.ppermute(flat[m], GRID, pairs)
        shard = got if shard is None else shard + got
    return shard


def cost(us):
    return pl.CostEstimate(flops=int(us * 1e9), bytes_accessed=int(us * 3e6), transcendentals=0)


def shards(kernel):
    tiles = kernel.reshape(2, T, T)
    me = lax.axis_index("row") * 16 + lax.axis_index("col")
    left = lax.ppermute(tiles[0], GRID, [(16, 0)])
    corner = lax.ppermute(tiles[0], GRID, [(17, 0)])
    first, w0 = pl.pallas_call(
        first_kernel,
        out_shape=[TILE, TILE],
        in_specs=[ANY],
        out_specs=[VMEM, VMEM],
        scratch_shapes=[pltpu.SemaphoreType.DMA],
        compiler_params=PARAMS,
        cost_estimate=cost(25),
        name="factor_first",
    )(tiles)
    tiles, w0 = lax.optimization_barrier((tiles, w0))
    shard = scatter_rows(tiles)
    rows = lax.all_gather(shard, "col", axis=0, tiled=True)
    shard, w0 = lax.optimization_barrier((shard, w0))
    w0_got = lax.ppermute(w0, GRID, [(0, 16)])
    w1 = pl.pallas_call(
        second_kernel,
        out_shape=TILE,
        in_specs=[VMEM] * 3,
        out_specs=VMEM,
        scratch_shapes=[pltpu.VMEM((T, T), f32), pltpu.VMEM((T, T), f32), PARTS, PARTS],
        compiler_params=PARAMS,
        cost_estimate=cost(30),
        name="factor_second",
    )(left, corner, w0)
    w1_cut = cut_out(w1, W_PIECES)
    w1_got = [lax.ppermute(w1_cut[k], GRID, [(0, 16)]) for k in (0, 2)]
    tiles, w0_got, w1 = lax.optimization_barrier((tiles, w0_got, w1))
    shard = scatter_cols(tiles)
    cols = lax.all_gather(shard, "row", axis=0, tiled=True)
    shard, w0_got = lax.optimization_barrier((shard, w0_got))
    panel = pl.pallas_call(
        panel_kernel,
        out_shape=TILE,
        in_specs=[ANY, VMEM],
        out_specs=VMEM,
        scratch_shapes=[pltpu.VMEM((T, T), f32), PARTS, PARTS, pltpu.SemaphoreType.DMA],
        compiler_params=PARAMS,
        cost_estimate=cost(5),
        name="panel_product",
    )(tiles, w0_got)
    w0_cut = cut_out(w0_got, W_PIECES)
    l_cut = cut_out(panel, L_PIECES)
    moved = []
    for k in (0, 2):
        moved += spread_early(w0_cut[k], w0_cut[k + 1], me)
    for k in (0, 2):
        moved += spread_early(l_cut[k], l_cut[k + 1], me)
    for k in (0, 2):
        moved += spread_late(w1_got[k // 2], w1_cut[k + 1], me)
    out = pl.pallas_call(
        last_kernel,
        out_shape=jax.ShapeDtypeStruct((2, T, T), f32),
        in_specs=[ANY] * 18,
        out_specs=ANY,
        scratch_shapes=[pltpu.VMEM((T, 3 * T), f32)] * 2
        + [pltpu.VMEM((T, T), f32)] * 3
        + [pltpu.VMEM((2, T, T), f32)]
        + [pltpu.VMEM((T, 3 * T), bf16)] * 2
        + [pltpu.VMEM((2 * T, 3 * T), bf16)] * 2
        + [pltpu.VMEM((T, 2 * T), f32), pltpu.VMEM((2, T, T), bf16), pltpu.VMEM((T, 2 * T), bf16)]
        + [pltpu.SemaphoreType.DMA((40,))],
        compiler_params=PARAMS,
        cost_estimate=cost(25),
        name="solve_and_update",
    )(tiles, rows, cols, first, w0, w0_got, *moved)
    return out.reshape(kernel.shape)


def solution(mesh):
    spec = P(None, "row", None, "col", None, None)
    return jax.shard_map(shards, mesh=mesh, in_specs=(spec,), out_specs=spec, check_vma=False)
```

```python
import functools

import jax
import jax.numpy as jnp
from jax import lax
from jax.experimental import pallas as pl
from jax.experimental.pallas import tpu as pltpu
from jax.sharding import PartitionSpec as P

f32 = jnp.float32
bf16 = jnp.bfloat16
T = 640
B = 128
NB = T // B
SG = 32
HIGHEST = lax.Precision.HIGHEST
NT = (((1,), (1,)), ((), ()))
TN = (((0,), (0,)), ((), ()))


def split3(x):
    high = x.astype(bf16)
    rest = x - high.astype(f32)
    mid = rest.astype(bf16)
    low = (rest - mid.astype(f32)).astype(bf16)
    return high, mid, low


def left6(parts, axis):
    h, m, l = parts
    return jnp.concatenate([h, h, m, m, h, l], axis)


def right6(parts):
    h, m, l = parts
    return jnp.concatenate([h, m, h, m, l, h], 0)


def dot6(left, right):
    return jnp.dot(left, right, preferred_element_type=f32)


def row_of(x, m):
    return jnp.broadcast_to(x[m : m + 1, :], x.shape)


def factor_block(block):
    groups = SG // 8
    row = lax.broadcasted_iota(jnp.int32, (B, B), 0)
    col = lax.broadcasted_iota(jnp.int32, (B, B), 1)
    unit = jnp.where(row == col, 1.0, 0.0)
    sub = lax.broadcasted_iota(jnp.int32, (8, B), 0)
    count = B // SG
    work = [
        jnp.concatenate([block[s * SG : (s + 1) * SG], unit[s * SG : (s + 1) * SG]], 1)
        for s in range(count)
    ]
    uppers, inverses = [], []
    for s in range(count):
        u = [work[s][8 * h : 8 * h + 8, :B] for h in range(groups)]
        w = [work[s][8 * h : 8 * h + 8, B:] for h in range(groups)]
        for g in range(groups):
            base = s * SG + 8 * g
            c = [
                [jnp.broadcast_to(u[h][:, base + m : base + m + 1], (8, B)) for m in range(8)]
                if h >= g
                else None
                for h in range(groups)
            ]
            scale = jnp.zeros((8, B), f32)
            for m in range(8):
                pivot = row_of(c[g][m], m)
                inverse = pltpu.reciprocal(pivot)
                scale = jnp.where(sub == m, lax.rsqrt(pivot), scale)
                u_row = row_of(u[g], m) * inverse
                w_row = row_of(w[g], m) * inverse
                c_row = [row_of(c[g][k], m) * inverse if k > m else None for k in range(8)]
                for h in range(g, groups):
                    factor = c[h][m]
                    if h == g:
                        factor = jnp.where(sub > m, factor, 0.0)
                    for k in range(m + 1, 8):
                        c[h][k] = c[h][k] - factor * c_row[k]
                    u[h] = u[h] - factor * u_row
                    w[h] = w[h] - factor * w_row
            u[g] = u[g] * scale
            w[g] = w[g] * scale
        upper = jnp.concatenate(u, 0)
        inverse = jnp.concatenate(w, 0)
        here = lax.broadcasted_iota(jnp.int32, (SG, B), 0) + s * SG
        upper = jnp.where(lax.broadcasted_iota(jnp.int32, (SG, B), 1) >= here, upper, 0.0)
        uppers.append(upper)
        inverses.append(inverse)
        if s < count - 1:
            left = left6(split3(upper[:, (s + 1) * SG :]), 0)
            right = right6(split3(jnp.concatenate([upper, inverse], 1)))
            change = lax.dot_general(left, right, TN, preferred_element_type=f32)
            for t in range(s + 1, count):
                work[t] = work[t] - change[(t - s - 1) * SG : (t - s) * SG]
    return jnp.concatenate(uppers, 0), jnp.concatenate(inverses, 0)


def factor_tile(read, lower_ref, inverse_ref):
    panel = [read(i) for i in range(NB)]
    aug = [None] * NB
    for i in range(NB):
        for j in range(i + 1, NB):
            lower_ref[i * B : (i + 1) * B, j * B : (j + 1) * B] = jnp.zeros((B, B), f32)
            inverse_ref[i * B : (i + 1) * B, j * B : (j + 1) * B] = jnp.zeros((B, B), f32)
    for b in range(NB):
        upper, inv = factor_block(panel[b][:, :B])
        rows = slice(b * B, (b + 1) * B)
        lower_ref[rows, rows] = upper.T
        inverse_ref[rows, rows] = inv
        left = left6(split3(inv), 1)
        if b > 0:
            w_left = dot6(left, right6(split3(aug[b])))
            inverse_ref[rows, : b * B] = w_left
            w_all = jnp.concatenate([w_left, inv], 1)
        else:
            w_all = inv
        if b == NB - 1:
            break
        w_parts = right6(split3(w_all))
        pieces = [
            dot6(left, right6(split3(panel[b][:, (i - b) * B : (i - b + 1) * B])))
            for i in range(b + 1, NB)
        ]
        u_parts = right6(split3(jnp.concatenate(pieces, 1)))
        for i in range(b + 1, NB):
            off = (i - b) * B
            turned = pieces[i - b - 1].T
            lower_ref[i * B : (i + 1) * B, rows] = turned
            left_i = left6(split3(turned), 1)
            panel[i] = panel[i] - dot6(left_i, u_parts[:, off - B :])
            grown = -dot6(left_i, w_parts)
            if b > 0:
                grown = jnp.concatenate([aug[i] + grown[:, : b * B], grown[:, b * B :]], 1)
            aug[i] = grown


def at_root():
    return (lax.axis_index("row") == 0) & (lax.axis_index("col") == 0)


FOLD = (
    ((512, 128, 640, 0),),
    ((384, 128, 512, 0), (0, 128, 128, 512)),
    ((256, 128, 384, 0), (128, 128, 256, 384)),
)
PLAIN = ((0, 0), (1, 128), (2, 256))


def fold_copies(tile, folded, sems, out, halves=False):
    found = []
    for p, pieces in enumerate(FOLD):
        for row, rows, width, at in pieces:
            if not halves:
                spots = [(row, rows, p * B)]
            elif p < 2:
                spots = [(row, rows, p * 192)]
            else:
                spots = [(row, 64, 128), (row + 64, 64, 320)]
            for first, count, place_at in spots:
                here = tile.at[pl.ds(first, count), pl.ds(0, width)]
                there = folded.at[pl.ds(place_at, count), pl.ds(at, width)]
                src, dst = (here, there) if out else (there, here)
                found.append(pltpu.make_async_copy(src, dst, sems.at[len(found)]))
    return found


def clear_gaps(ref):
    ref[:B, B : 2 * B] = jnp.zeros((B, B), f32)
    ref[2 * B : 3 * B, 3 * B : 4 * B] = jnp.zeros((B, B), f32)


def run(copies):
    for one in copies:
        one.start()
    for one in copies:
        one.wait()


def first_kernel(tiles_ref, lower_ref, fold_ref, inverse, sem):
    @pl.when(at_root())
    def _():
        run([pltpu.make_async_copy(tiles_ref.at[0], lower_ref, sem)])
        blocks = [lower_ref[i * B : (i + 1) * B, i * B :] for i in range(NB)]
        factor_tile(lambda i: blocks[i], lower_ref, inverse)
        for p, pieces in enumerate(FOLD):
            for row, rows, width, at in pieces:
                fold_ref[p * B : (p + 1) * B, at : at + width] = inverse[row : row + rows, :width]


def split2(x):
    high = x.astype(bf16)
    return high, (x - high.astype(f32)).astype(bf16)


def keep_parts(ref, parts):
    for i in range(NB):
        rows = slice(i * B, (i + 1) * B)
        for n, part in enumerate(split3(ref[rows, :])):
            parts[rows, n * T : (n + 1) * T] = part


def stacked(parts, order, rows, depth):
    return jnp.concatenate([parts[rows, n * T : n * T + depth] for n in order], 1)


LEFT = (0, 0, 1, 1, 0, 2)
RIGHT = (0, 1, 0, 1, 2, 0)
GROUPS = ((0, 256, 256), (256, 256, 512), (512, 128, 640))


def times_inverse(tile_ref, inverse_ref, out_ref, tile_parts, inverse_parts):
    keep_parts(tile_ref, tile_parts)
    keep_parts(inverse_ref, inverse_parts)
    for first, count, depth in GROUPS:
        rows = slice(first, first + count)
        left = stacked(tile_parts, LEFT, slice(None), depth)
        right = stacked(inverse_parts, RIGHT, rows, depth)
        out_ref[:, rows] = lax.dot_general(left, right, NT, preferred_element_type=f32)


def second_kernel(
    left_ref, corner_ref, fold_ref, out_ref, left, corner, inverse, panel, lower, parts, more, sems
):
    @pl.when(at_root())
    def _():
        clear_gaps(inverse)
        run(
            fold_copies(inverse, fold_ref, sems, False)
            + [
                pltpu.make_async_copy(left_ref, left, sems.at[14]),
                pltpu.make_async_copy(corner_ref, corner, sems.at[15]),
            ]
        )
        times_inverse(left, inverse, panel, parts, more)
        keep_parts(panel, parts)
        for i in range(NB):
            one = stacked(parts, LEFT, slice(i * B, (i + 1) * B), T)
            two = stacked(parts, RIGHT, slice(i * B, T), T)
            change = lax.dot_general(one, two, NT, preferred_element_type=f32)
            lower[i * B : (i + 1) * B, i * B :] = corner[i * B : (i + 1) * B, i * B :] - change
        blocks = [lower[i * B : (i + 1) * B, i * B :] for i in range(NB)]
        factor_tile(lambda i: blocks[i], lower, inverse)
        run(fold_copies(inverse, out_ref, sems, True, True))


def panel_kernel(tiles_ref, fold_ref, out_ref, tile, inverse, panel, parts, more, sems):
    r = lax.axis_index("row")
    c = lax.axis_index("col")

    @pl.when(r + c == 1)
    def _():
        clear_gaps(inverse)
        run(
            fold_copies(inverse, fold_ref, sems, False)
            + [pltpu.make_async_copy(tiles_ref.at[0], tile, sems.at[15])]
        )

        @pl.when(c == 1)
        def _():
            tile[...] = tile[...].T

        times_inverse(tile, inverse, panel, parts, more)
        run([pltpu.make_async_copy(panel, out_ref, sems.at[15])])


CHUNKS = ((0, 512), (512, 512), (1024, 512), (1536, 384))

def triangular(w_ref, parts, xh, xl, emit):
    high, low = split2(w_ref[...])
    parts[0] = high
    parts[1] = low
    for n, width in CHUNKS:
        for first, count, depth in GROUPS:
            wh = parts[0, first : first + count, :depth]
            wl = parts[1, first : first + count, :depth]
            top = xh[:depth, n : n + width]
            both = dot6(jnp.concatenate([wh, wl], 0), top)
            rest = dot6(wh, xl[:depth, n : n + width])
            emit(first, count, n, width, both[:count] + both[count:] + rest)


def last_kernel(*refs):
    tiles_ref, rows_ref, cols_ref, first_ref, own_ref, got_ref = refs[:6]
    moved = refs[6:18]
    out_ref = refs[18]
    x0, x1, wa, la, wb, tile, xh, xl, yh, yl, yf, parts, lparts, sems = refs[19:]
    r = lax.axis_index("row")
    c = lax.axis_index("col")
    odd = lax.rem(r, 2) == 1
    inner = c > 0
    used = iter(range(40))

    def copy(src, dst, sem=None):
        return pltpu.make_async_copy(src, dst, sems.at[next(used) if sem is None else sem])

    first_x = [
        copy(rows_ref.at[pl.ds(0, T)], x0.at[:, pl.ds(0, T)]),
        copy(rows_ref.at[pl.ds(2 * T, T)], x0.at[:, pl.ds(T, T)]),
        copy(cols_ref.at[pl.ds(0, T)], x0.at[:, pl.ds(2 * T, T)]),
    ]
    second_x = [
        copy(rows_ref.at[pl.ds(T, T)], x1.at[:, pl.ds(0, T)]),
        copy(rows_ref.at[pl.ds(3 * T, T)], x1.at[:, pl.ds(T, T)]),
        copy(cols_ref.at[pl.ds(T, T)], x1.at[:, pl.ds(2 * T, T)]),
    ]
    old = [copy(tiles_ref.at[a], tile.at[a]) for a in range(2)]
    new = [copy(tile.at[a], out_ref.at[a]) for a in range(2)]
    lower = copy(first_ref, tile.at[0], next(used))

    def unfold(dst, p, src, ids, part=None):
        found = []
        for row, rows, width, at in FOLD[p]:
            if part is not None:
                row, rows = row + 64 * part, 64
            got = src.at[pl.ds(0, rows), pl.ds(at, width)]
            found.append(copy(got, dst.at[pl.ds(row, rows), pl.ds(0, width)], ids[len(found)]))
        return found

    def take(n):
        return [next(used) for _ in range(n)]

    def both(k):
        cur, swap = moved[2 * k : 2 * k + 2]
        return (swap, cur), (cur, swap)

    def l_copy(n, src, ids):
        return [copy(src, la.at[pl.ds(n * B, B)], ids[0])]

    w0_ids, l_ids, w1_ids = [take(2) for _ in range(3)], [take(1) for _ in range(5)], [take(2) for _ in range(4)]

    def w0_copies(sources):
        return [one for p in range(3) for one in unfold(wa, p, sources[p], w0_ids[p])]

    def w0_case(side):
        return w0_copies([both(0)[side][0], both(0)[side][1], both(1)[side][0]])

    def l_case(side):
        sources = [both(1)[side][1], *both(2)[side], *both(3)[side]]
        return [one for n in range(5) for one in l_copy(n, sources[n], l_ids[n])]

    def w1_case(side):
        pieces, halves = both(4)[side], both(5)[side]
        found = [one for p in range(2) for one in unfold(wb, p, pieces[p], w1_ids[p])]
        return found + [one for h in range(2) for one in unfold(wb, 2, halves[h], w1_ids[2 + h], h)]

    def whole(ref):
        return w0_copies([ref.at[pl.ds(p * B, B)] for p in range(3)])

    def start(copies):
        for one in copies:
            one.start()

    def wait(copies):
        for one in copies:
            one.wait()

    for one in first_x:
        one.start()

    clear_gaps(wa)

    @pl.when((c == 0) & (r == 0))
    def _():
        start(whole(own_ref))

    @pl.when((c == 0) & (r == 1))
    def _():
        start(whole(got_ref))

    far = (c > 0) | (r > 1)
    for side in range(2):

        @pl.when(far & (odd if side else jnp.logical_not(odd)))
        def _():
            start(w0_case(side))

    @pl.when(inner)
    def _():
        start(second_x)
        clear_gaps(wb)
        start(old)

    for side in range(2):

        @pl.when(inner & (odd if side else jnp.logical_not(odd)))
        def _():
            start(l_case(side))
            start(w1_case(side))

    for one in first_x:
        one.wait()

    def cut(i, carry):
        rows = pl.ds(pl.multiple_of(i * B, B), B)
        xh[rows, :], xl[rows, :] = split2(x0[rows, :])
        return carry

    lax.fori_loop(0, NB, cut, 0)

    wait(w0_case(0))

    def emit(base):
        def store(first, count, n, width, y):
            rows = slice(base + first, base + first + count)
            yh[rows, n : n + width], yl[rows, n : n + width] = split2(y)
            keep = min(width, 2 * T - n)
            if keep > 0:
                yf[first : first + count, n : n + keep] = y[:, :keep]

        return store

    triangular(wa, parts, xh, xl, emit(0))

    @pl.when(inner)
    def _():
        for one in second_x:
            one.wait()
        wait(l_case(0))
        lparts[:, :T], lparts[:, T:] = split2(la[...])

        def step(i, carry):
            at = pl.ds(pl.multiple_of(i * T, B), T)
            left = jnp.concatenate([lparts[:, :T], lparts[:, :T], lparts[:, T:]], 1)
            high = yh[:T, at]
            right = jnp.concatenate([high, yl[:T, at], high], 0)
            xh[:, at], xl[:, at] = split2(x1[:, at] - dot6(left, right))
            return carry

        lax.fori_loop(0, 3, step, 0)
        wait(w1_case(0))
        triangular(wb, parts, xh, xl, emit(T))
        for one in old:
            one.wait()

    @pl.when(r == 1)
    def _():
        yh[T:, :T] = jnp.zeros((T, T), bf16)
        yl[T:, :T] = jnp.zeros((T, T), bf16)

    for a in range(2):
        top = r + 8 * a

        @pl.when((c > 1) & (top > 0))
        def _():
            def step(i, carry):
                at = pl.ds(pl.multiple_of(a * T + i * B, B), B)
                rows = pl.ds(pl.multiple_of(i * B, B), B)
                high = yh[:, at]
                left = jnp.concatenate([high, yl[:, at]], 1)
                both = lax.dot_general(left, yh[:, 2 * T :], TN, preferred_element_type=f32)
                rest = lax.dot_general(high, yl[:, 2 * T :], TN, preferred_element_type=f32)
                tile[a, rows, :] = tile[a, rows, :] - (both[:B] + both[B:] + rest)
                return carry

            lax.fori_loop(0, NB, step, 0)

        @pl.when((top == 0) & (c == 0))
        def _():
            lower.start()
            lower.wait()

        @pl.when((top > 0) & (c < 2))
        def _():
            turned = yf[:, a * T : (a + 1) * T].T
            row = lax.broadcasted_iota(jnp.int32, (T, T), 0)
            col = lax.broadcasted_iota(jnp.int32, (T, T), 1)
            tile[a] = jnp.where((top == 1) & (c == 1) & (col > row), 0.0, turned)

        new[a].start()
    for one in new:
        one.wait()


VMEM = pl.BlockSpec(memory_space=pltpu.VMEM)
ANY = pl.BlockSpec(memory_space=pl.ANY)
PARAMS = pltpu.CompilerParams(vmem_limit_bytes=56 << 20)
TILE = jax.ShapeDtypeStruct((T, T), f32)
PARTS = pltpu.VMEM((T, 3 * T), bf16)
GRID = ("row", "col")


def place(x, y, z, core):
    return (y * 2 + core) * 16 + x * 4 + z


def branches(core, start, order):
    def move(chip, axis, by):
        return tuple((v + by) % 4 if n == axis else v for n, v in enumerate(chip))

    have, rounds = [start], []
    for axis in order:
        new = [move(chip, axis, 1) for chip in have]
        rounds.append(list(zip(have, new)))
        rounds.append(
            [(chip, move(chip, axis, -1)) for chip in have] + [(chip, move(chip, axis, 1)) for chip in new]
        )
        have = have + new + [dst for _, dst in rounds[-1]]
    return [[(place(*src, core), place(*dst, core)) for src, dst in pairs] for pairs in rounds]


def trees():
    first = [
        one + [pair for pair in two if pair[1] != 0]
        for one, two in zip(branches(1, (0, 0, 0), (0, 2, 1)), branches(0, (0, 0, 1), (1, 0, 2)))
    ]
    second = [
        one + two for one, two in zip(branches(1, (0, 1, 0), (0, 2, 1)), branches(0, (0, 1, 0), (1, 0, 2)))
    ]
    chips = [(x, y, z) for x in range(4) for y in range(4) for z in range(4)]
    swap = [(place(*chip, k), place(*chip, 1 - k)) for chip in chips for k in range(2)]
    return first + [swap], second + [swap]


TIE = 9


def wave(curs, late, rows):
    plans = [trees()[k >= late] for k in range(len(curs))]
    curs, count, last = list(curs), len(curs), len(plans[0]) - 1
    pairs, going = [None] * count, {}
    for t in range(count + last + 1):
        arrived, going = going, {}
        for k, got in sorted(arrived.items()):
            after = k + 1 if k >= late else k + 2
            if after < count and (after >= late) == (k >= late):
                got, curs[after] = lax.optimization_barrier((got, curs[after]))
            if t - 1 - k == last:
                pairs[k] = (curs[k], got)
            else:
                curs[k] = curs[k] + got
        if t == TIE:
            rows, curs[-1] = lax.optimization_barrier((rows, curs[-1]))
        for k in range(count):
            if 0 <= t - k <= last:
                going[k] = lax.ppermute(curs[k], GRID, plans[k][t - k])
    return [one for pair in pairs for one in pair], rows


def scatter_rows(tiles):
    flat = tiles[0].reshape(4, T // 4, T)
    shard = None
    for m in range(4):
        pairs = [
            (h * 16 + j, (j % 8) * 16 + (j // 8) * 8 + h * 4 + m)
            for j in range(1, 16)
            for h in range(2)
        ]
        got = lax.ppermute(flat[m], GRID, pairs)
        shard = got if shard is None else shard + got
    return shard


def scatter_cols(tiles):
    flat = tiles[0].reshape(4, T // 4, T)
    shard = None
    for m in range(4):
        pairs = [(h * 16 + c, (h * 4 + m) * 16 + c) for c in range(2, 16) for h in range(2)]
        got = lax.ppermute(flat[m], GRID, pairs)
        shard = got if shard is None else shard + got
    return shard


def cost(us):
    return pl.CostEstimate(flops=int(us * 1e9), bytes_accessed=int(us * 3e6), transcendentals=0)


SHARD = (T // 4, T)
FOLDED = jax.ShapeDtypeStruct((3 * B, T), f32)
WHOLE = pltpu.VMEM((T, T), f32)
SEMS = pltpu.SemaphoreType.DMA((16,))


def kernel_call(body, out_shape, scratch, us, name, count):
    many = isinstance(out_shape, list)
    return pl.pallas_call(
        body,
        out_shape=out_shape,
        in_specs=[ANY] * count,
        out_specs=[ANY] * len(out_shape) if many else ANY,
        scratch_shapes=scratch,
        compiler_params=PARAMS,
        cost_estimate=cost(us),
        name=name,
    )


def shards(kernel):
    tiles = kernel.reshape(2, T, T)
    me = lax.axis_index("row") * 16 + lax.axis_index("col")
    left = lax.ppermute(tiles[0], GRID, [(16, 0)])
    corner = lax.ppermute(tiles[0], GRID, [(17, 0)])

    def factor(tiles):
        return tuple(
            pl.pallas_call(
                first_kernel,
                out_shape=[TILE, FOLDED],
                in_specs=[ANY],
                out_specs=[VMEM, VMEM],
                scratch_shapes=[WHOLE, pltpu.SemaphoreType.DMA],
                compiler_params=PARAMS,
                cost_estimate=cost(25),
                name="factor_first",
            )(tiles)
        )

    def skip(tiles):
        return jnp.zeros((T, T), f32), jnp.zeros((3 * B, T), f32)

    first, fold0 = lax.cond(me == 0, factor, skip, tiles)
    tiles, fold0 = lax.optimization_barrier((tiles, fold0))
    row_shard = scatter_rows(tiles)
    row_shard, fold0 = lax.optimization_barrier((row_shard, fold0))
    rows = lax.all_gather(row_shard, "col", axis=0, tiled=True)
    fold0_one = lax.ppermute(fold0, GRID, [(0, 16)])
    fold0_two = lax.ppermute(fold0, GRID, [(0, 1)])
    fold1 = kernel_call(
        second_kernel, FOLDED, [WHOLE] * 5 + [PARTS, PARTS, SEMS], 30, "factor_second", 3
    )(left, corner, fold0)
    one = lax.ppermute(fold1[:192], GRID, [(0, place(0, 1, 0, 1))])
    two = lax.ppermute(fold1[192:], GRID, [(0, place(0, 1, 0, 0))])
    fold0_one, fold0_two, one, two, tiles = lax.optimization_barrier(
        (fold0_one, fold0_two, one, two, tiles)
    )
    fold0_got = fold0_one + fold0_two
    col_shard = scatter_cols(tiles)
    col_shard, fold0_got, tiles = lax.optimization_barrier((col_shard, fold0_got, tiles))
    cols = lax.all_gather(col_shard, "row", axis=0, tiled=True)
    panel = kernel_call(
        panel_kernel, TILE, [WHOLE] * 3 + [PARTS, PARTS, SEMS], 5, "panel_product", 2
    )(tiles, fold0_got)
    pieces = [fold0_got[p * B : (p + 1) * B] for p in range(3)]
    pieces += [panel[n * B : (n + 1) * B] for n in range(5)]
    curs = [
        jnp.where(me == 16, pieces[2 * k], jnp.where(me == 1, pieces[2 * k + 1], 0.0)) for k in range(4)
    ]
    both = one + two
    moved, rows = wave(curs + [both[:B], both[B:]], 4, rows)
    out = pl.pallas_call(
        last_kernel,
        out_shape=jax.ShapeDtypeStruct((2, T, T), f32),
        in_specs=[ANY] * 18,
        out_specs=ANY,
        scratch_shapes=[pltpu.VMEM((T, 3 * T), f32)] * 2
        + [WHOLE] * 3
        + [pltpu.VMEM((2, T, T), f32)]
        + [pltpu.VMEM((T, 3 * T), bf16)] * 2
        + [pltpu.VMEM((2 * T, 3 * T), bf16)] * 2
        + [pltpu.VMEM((T, 2 * T), f32), pltpu.VMEM((2, T, T), bf16), pltpu.VMEM((T, 2 * T), bf16)]
        + [pltpu.SemaphoreType.DMA((40,))],
        compiler_params=PARAMS,
        cost_estimate=cost(25),
        name="solve_and_update",
    )(tiles, rows, cols, first, fold0, fold0_got, *moved)
    return out.reshape(kernel.shape)


def solution(mesh):
    spec = P(None, "row", None, "col", None, None)
    return jax.shard_map(shards, mesh=mesh, in_specs=(spec,), out_specs=spec, check_vma=False)
```

```python
import functools

import jax
import jax.numpy as jnp
from jax import lax
from jax.experimental import pallas as pl
from jax.experimental.pallas import tpu as pltpu
from jax.sharding import PartitionSpec as P

f32 = jnp.float32
bf16 = jnp.bfloat16
T = 640
B = 128
NB = T // B
SG = 32
HIGHEST = lax.Precision.HIGHEST
NT = (((1,), (1,)), ((), ()))
TN = (((0,), (0,)), ((), ()))


def split3(x):
    high = x.astype(bf16)
    rest = x - high.astype(f32)
    mid = rest.astype(bf16)
    low = (rest - mid.astype(f32)).astype(bf16)
    return high, mid, low


def left6(parts, axis):
    h, m, l = parts
    return jnp.concatenate([h, h, m, m, h, l], axis)


def right6(parts):
    h, m, l = parts
    return jnp.concatenate([h, m, h, m, l, h], 0)


def dot6(left, right):
    return jnp.dot(left, right, preferred_element_type=f32)


def row_of(x, m):
    return jnp.broadcast_to(x[m : m + 1, :], x.shape)


def factor_block(block):
    groups = SG // 8
    row = lax.broadcasted_iota(jnp.int32, (B, B), 0)
    col = lax.broadcasted_iota(jnp.int32, (B, B), 1)
    unit = jnp.where(row == col, 1.0, 0.0)
    sub = lax.broadcasted_iota(jnp.int32, (8, B), 0)
    count = B // SG
    work = [
        jnp.concatenate([block[s * SG : (s + 1) * SG], unit[s * SG : (s + 1) * SG]], 1)
        for s in range(count)
    ]
    uppers, inverses = [], []
    for s in range(count):
        u = [work[s][8 * h : 8 * h + 8, :B] for h in range(groups)]
        w = [work[s][8 * h : 8 * h + 8, B:] for h in range(groups)]
        for g in range(groups):
            base = s * SG + 8 * g
            c = [
                [jnp.broadcast_to(u[h][:, base + m : base + m + 1], (8, B)) for m in range(8)]
                if h >= g
                else None
                for h in range(groups)
            ]
            scale = jnp.zeros((8, B), f32)
            for m in range(8):
                pivot = row_of(c[g][m], m)
                inverse = pltpu.reciprocal(pivot)
                scale = jnp.where(sub == m, lax.rsqrt(pivot), scale)
                u_row = row_of(u[g], m) * inverse
                w_row = row_of(w[g], m) * inverse
                c_row = [row_of(c[g][k], m) * inverse if k > m else None for k in range(8)]
                for h in range(g, groups):
                    factor = c[h][m]
                    if h == g:
                        factor = jnp.where(sub > m, factor, 0.0)
                    for k in range(m + 1, 8):
                        c[h][k] = c[h][k] - factor * c_row[k]
                    u[h] = u[h] - factor * u_row
                    w[h] = w[h] - factor * w_row
            u[g] = u[g] * scale
            w[g] = w[g] * scale
        upper = jnp.concatenate(u, 0)
        inverse = jnp.concatenate(w, 0)
        here = lax.broadcasted_iota(jnp.int32, (SG, B), 0) + s * SG
        upper = jnp.where(lax.broadcasted_iota(jnp.int32, (SG, B), 1) >= here, upper, 0.0)
        uppers.append(upper)
        inverses.append(inverse)
        if s < count - 1:
            left = left6(split3(upper[:, (s + 1) * SG :]), 0)
            right = right6(split3(jnp.concatenate([upper, inverse], 1)))
            change = lax.dot_general(left, right, TN, preferred_element_type=f32)
            for t in range(s + 1, count):
                work[t] = work[t] - change[(t - s - 1) * SG : (t - s) * SG]
    return jnp.concatenate(uppers, 0), jnp.concatenate(inverses, 0)


def factor_tile(read, lower_ref, inverse_ref):
    panel = [read(i) for i in range(NB)]
    aug = [None] * NB
    for i in range(NB):
        for j in range(i + 1, NB):
            lower_ref[i * B : (i + 1) * B, j * B : (j + 1) * B] = jnp.zeros((B, B), f32)
            inverse_ref[i * B : (i + 1) * B, j * B : (j + 1) * B] = jnp.zeros((B, B), f32)
    for b in range(NB):
        upper, inv = factor_block(panel[b][:, :B])
        rows = slice(b * B, (b + 1) * B)
        lower_ref[rows, rows] = upper.T
        inverse_ref[rows, rows] = inv
        left = left6(split3(inv), 1)
        if b > 0:
            w_left = dot6(left, right6(split3(aug[b])))
            inverse_ref[rows, : b * B] = w_left
            w_all = jnp.concatenate([w_left, inv], 1)
        else:
            w_all = inv
        if b == NB - 1:
            break
        w_parts = right6(split3(w_all))
        pieces = [
            dot6(left, right6(split3(panel[b][:, (i - b) * B : (i - b + 1) * B])))
            for i in range(b + 1, NB)
        ]
        u_parts = right6(split3(jnp.concatenate(pieces, 1)))
        for i in range(b + 1, NB):
            off = (i - b) * B
            turned = pieces[i - b - 1].T
            lower_ref[i * B : (i + 1) * B, rows] = turned
            left_i = left6(split3(turned), 1)
            panel[i] = panel[i] - dot6(left_i, u_parts[:, off - B :])
            grown = -dot6(left_i, w_parts)
            if b > 0:
                grown = jnp.concatenate([aug[i] + grown[:, : b * B], grown[:, b * B :]], 1)
            aug[i] = grown


def at_root():
    return (lax.axis_index("row") == 0) & (lax.axis_index("col") == 0)


FOLD = (
    ((512, 128, 640, 0),),
    ((384, 128, 512, 0), (0, 128, 128, 512)),
    ((256, 128, 384, 0), (128, 128, 256, 384)),
)
PLAIN = ((0, 0), (1, 128), (2, 256))


def fold_copies(tile, folded, sems, out, halves=False):
    found = []
    for p, pieces in enumerate(FOLD):
        for row, rows, width, at in pieces:
            if not halves:
                spots = [(row, rows, p * B)]
            elif p < 2:
                spots = [(row, rows, p * 192)]
            else:
                spots = [(row, 64, 128), (row + 64, 64, 320)]
            for first, count, place_at in spots:
                here = tile.at[pl.ds(first, count), pl.ds(0, width)]
                there = folded.at[pl.ds(place_at, count), pl.ds(at, width)]
                src, dst = (here, there) if out else (there, here)
                found.append(pltpu.make_async_copy(src, dst, sems.at[len(found)]))
    return found


def clear_gaps(ref):
    ref[:B, B : 2 * B] = jnp.zeros((B, B), f32)
    ref[2 * B : 3 * B, 3 * B : 4 * B] = jnp.zeros((B, B), f32)


def run(copies):
    for one in copies:
        one.start()
    for one in copies:
        one.wait()


def first_kernel(tiles_ref, lower_ref, fold_ref, inverse, sem):
    @pl.when(at_root())
    def _():
        run([pltpu.make_async_copy(tiles_ref.at[0], lower_ref, sem)])
        blocks = [lower_ref[i * B : (i + 1) * B, i * B :] for i in range(NB)]
        factor_tile(lambda i: blocks[i], lower_ref, inverse)
        for p, pieces in enumerate(FOLD):
            for row, rows, width, at in pieces:
                fold_ref[p * B : (p + 1) * B, at : at + width] = inverse[row : row + rows, :width]


def split2(x):
    high = x.astype(bf16)
    return high, (x - high.astype(f32)).astype(bf16)


def keep_parts(ref, parts):
    for i in range(NB):
        rows = slice(i * B, (i + 1) * B)
        for n, part in enumerate(split3(ref[rows, :])):
            parts[rows, n * T : (n + 1) * T] = part


def stacked(parts, order, rows, depth):
    return jnp.concatenate([parts[rows, n * T : n * T + depth] for n in order], 1)


LEFT = (0, 0, 1, 1, 0, 2)
RIGHT = (0, 1, 0, 1, 2, 0)
GROUPS = ((0, 256, 256), (256, 256, 512), (512, 128, 640))


def times_inverse(tile_ref, inverse_ref, out_ref, tile_parts, inverse_parts):
    keep_parts(tile_ref, tile_parts)
    keep_parts(inverse_ref, inverse_parts)
    for first, count, depth in GROUPS:
        rows = slice(first, first + count)
        left = stacked(tile_parts, LEFT, slice(None), depth)
        right = stacked(inverse_parts, RIGHT, rows, depth)
        out_ref[:, rows] = lax.dot_general(left, right, NT, preferred_element_type=f32)


def second_kernel(
    left_ref, corner_ref, fold_ref, out_ref, left, corner, inverse, panel, lower, parts, more, sems
):
    @pl.when(at_root())
    def _():
        clear_gaps(inverse)
        run(
            fold_copies(inverse, fold_ref, sems, False)
            + [
                pltpu.make_async_copy(left_ref, left, sems.at[14]),
                pltpu.make_async_copy(corner_ref, corner, sems.at[15]),
            ]
        )
        times_inverse(left, inverse, panel, parts, more)
        keep_parts(panel, parts)
        for i in range(NB):
            one = stacked(parts, LEFT, slice(i * B, (i + 1) * B), T)
            two = stacked(parts, RIGHT, slice(i * B, T), T)
            change = lax.dot_general(one, two, NT, preferred_element_type=f32)
            lower[i * B : (i + 1) * B, i * B :] = corner[i * B : (i + 1) * B, i * B :] - change
        blocks = [lower[i * B : (i + 1) * B, i * B :] for i in range(NB)]
        factor_tile(lambda i: blocks[i], lower, inverse)
        run(fold_copies(inverse, out_ref, sems, True, True))


def panel_kernel(tiles_ref, fold_ref, out_ref, tile, inverse, panel, parts, more, sems):
    r = lax.axis_index("row")
    c = lax.axis_index("col")

    @pl.when(r + c == 1)
    def _():
        clear_gaps(inverse)
        run(
            fold_copies(inverse, fold_ref, sems, False)
            + [pltpu.make_async_copy(tiles_ref.at[0], tile, sems.at[15])]
        )

        @pl.when(c == 1)
        def _():
            tile[...] = tile[...].T

        times_inverse(tile, inverse, panel, parts, more)
        run([pltpu.make_async_copy(panel, out_ref, sems.at[15])])


WIDE = 2048
CHUNK = 512


def triangular(w_ref, parts, xh, xl, emit):
    high, low = split2(w_ref[...])
    parts[0] = high
    parts[1] = low

    def step(n, carry):
        at = pl.ds(pl.multiple_of(n * CHUNK, CHUNK), CHUNK)
        for first, count, depth in GROUPS:
            wh = parts[0, first : first + count, :depth]
            wl = parts[1, first : first + count, :depth]
            top = xh[:depth, at]
            both = dot6(jnp.concatenate([wh, wl], 0), top)
            rest = dot6(wh, xl[:depth, at])
            emit(first, count, at, both[:count] + both[count:] + rest)
        return carry

    lax.fori_loop(0, WIDE // CHUNK, step, 0)


def last_kernel(*refs):
    tiles_ref, rows_ref, cols_ref, first_ref, own_ref, got_ref = refs[:6]
    moved = refs[6:18]
    out_ref = refs[18]
    x0, x1, wa, la, wb, tile, xh, xl, yh, yl, yf, parts, lparts, sems = refs[19:]
    r = lax.axis_index("row")
    c = lax.axis_index("col")
    odd = lax.rem(r, 2) == 1
    inner = c > 0
    used = iter(range(40))

    def copy(src, dst, sem=None):
        return pltpu.make_async_copy(src, dst, sems.at[next(used) if sem is None else sem])

    first_x = [
        copy(rows_ref.at[pl.ds(0, T)], x0.at[:, pl.ds(0, T)]),
        copy(rows_ref.at[pl.ds(2 * T, T)], x0.at[:, pl.ds(T, T)]),
        copy(cols_ref.at[pl.ds(0, T)], x0.at[:, pl.ds(2 * T, T)]),
    ]
    second_x = [
        copy(rows_ref.at[pl.ds(T, T)], x1.at[:, pl.ds(0, T)], 30),
        copy(rows_ref.at[pl.ds(3 * T, T)], x1.at[:, pl.ds(T, T)]),
        copy(cols_ref.at[pl.ds(T, T)], x1.at[:, pl.ds(2 * T, T)]),
    ]
    old = [copy(tiles_ref.at[a], tile.at[a]) for a in range(2)]
    new = [copy(tile.at[a], out_ref.at[a]) for a in range(2)]
    lower = copy(first_ref, tile.at[0], next(used))

    def unfold(dst, p, src, ids, part=None):
        found = []
        for row, rows, width, at in FOLD[p]:
            if part is not None:
                row, rows = row + 64 * part, 64
            got = src.at[pl.ds(0, rows), pl.ds(at, width)]
            found.append(copy(got, dst.at[pl.ds(row, rows), pl.ds(0, width)], ids[len(found)]))
        return found

    def take(n):
        return [next(used) for _ in range(n)]

    def both(k):
        cur, swap = moved[2 * k : 2 * k + 2]
        return (swap, cur), (cur, swap)

    def l_copy(n, src, ids):
        return [copy(src, la.at[pl.ds(n * B, B)], ids[0])]

    w0_ids, l_ids, w1_ids = [take(2) for _ in range(3)], [take(1) for _ in range(5)], [take(2) for _ in range(4)]

    def w0_copies(sources):
        return [one for p in range(3) for one in unfold(wa, p, sources[p], w0_ids[p])]

    def w0_case(side):
        return w0_copies([both(0)[side][0], both(0)[side][1], both(1)[side][0]])

    def l_case(side):
        sources = [both(1)[side][1], *both(2)[side], *both(3)[side]]
        return [one for n in range(5) for one in l_copy(n, sources[n], l_ids[n])]

    def w1_case(side):
        pieces, halves = both(4)[side], both(5)[side]
        found = [one for p in range(2) for one in unfold(wb, p, pieces[p], w1_ids[p])]
        return found + [one for h in range(2) for one in unfold(wb, 2, halves[h], w1_ids[2 + h], h)]

    def whole(ref):
        return w0_copies([ref.at[pl.ds(p * B, B)] for p in range(3)])

    def start(copies):
        for one in copies:
            one.start()

    def wait(copies):
        for one in copies:
            one.wait()

    for one in first_x:
        one.start()

    clear_gaps(wa)

    @pl.when((c == 0) & (r == 0))
    def _():
        start(whole(own_ref))

    @pl.when((c == 0) & (r == 1))
    def _():
        start(whole(got_ref))

    far = (c > 0) | (r > 1)
    for side in range(2):

        @pl.when(far & (odd if side else jnp.logical_not(odd)))
        def _():
            start(w0_case(side))

    @pl.when((r == 1) & (c == 1))
    def _():
        copy(tiles_ref.at[0], x1.at[:, pl.ds(0, T)], 30).start()

    @pl.when(inner & ((r != 1) | (c != 1)))
    def _():
        second_x[0].start()

    @pl.when(inner)
    def _():
        start(second_x[1:])
        clear_gaps(wb)
        start(old)

    for side in range(2):

        @pl.when(inner & (odd if side else jnp.logical_not(odd)))
        def _():
            start(l_case(side))
            start(w1_case(side))

    for one in first_x:
        one.wait()

    def cut(i, carry):
        rows = pl.ds(pl.multiple_of(i * B, B), B)
        xh[rows, : 3 * T], xl[rows, : 3 * T] = split2(x0[rows, :])
        return carry

    lax.fori_loop(0, NB, cut, 0)

    wait(w0_case(0))

    def emit(base):
        def store(first, count, at, y):
            rows = slice(base + first, base + first + count)
            yh[rows, at], yl[rows, at] = split2(y)
            yf[first : first + count, at] = y

        return store

    triangular(wa, parts, xh, xl, emit(0))

    @pl.when(inner)
    def _():
        for one in second_x:
            one.wait()
        wait(l_case(0))
        lparts[:, :T], lparts[:, T:] = split2(la[...])

        def step(i, carry):
            at = pl.ds(pl.multiple_of(i * T, B), T)
            left = jnp.concatenate([lparts[:, :T], lparts[:, :T], lparts[:, T:]], 1)
            high = yh[:T, at]
            right = jnp.concatenate([high, yl[:T, at], high], 0)
            xh[:, at], xl[:, at] = split2(x1[:, at] - dot6(left, right))
            return carry

        lax.fori_loop(0, 3, step, 0)
        wait(w1_case(0))
        triangular(wb, parts, xh, xl, emit(T))
        for one in old:
            one.wait()

    @pl.when(r == 1)
    def _():
        yh[T:, :T] = jnp.zeros((T, T), bf16)
        yl[T:, :T] = jnp.zeros((T, T), bf16)

    def update(n, carry):
        a = n // NB
        top = r + 8 * a

        @pl.when((c > 1) & (top > 0))
        def _():
            at = pl.ds(pl.multiple_of(n * B, B), B)
            rows = pl.ds(pl.multiple_of((n - a * NB) * B, B), B)
            high = yh[:, at]
            left = jnp.concatenate([high, yl[:, at]], 1)
            both = lax.dot_general(left, yh[:, 2 * T : 3 * T], TN, preferred_element_type=f32)
            rest = lax.dot_general(high, yl[:, 2 * T : 3 * T], TN, preferred_element_type=f32)
            tile[a, rows, :] = tile[a, rows, :] - (both[:B] + both[B:] + rest)

        @pl.when((top > 0) & (c < 2))
        def _():
            at = pl.ds(pl.multiple_of(n * B, B), B)
            rows = pl.ds(pl.multiple_of((n - a * NB) * B, B), B)
            row = lax.broadcasted_iota(jnp.int32, (B, T), 0) + (n - a * NB) * B
            col = lax.broadcasted_iota(jnp.int32, (B, T), 1)
            tile[a, rows, :] = jnp.where((top == 1) & (c == 1) & (col > row), 0.0, yf[:, at].T)

        return carry

    lax.fori_loop(0, 2 * NB, update, 0)

    @pl.when((r == 0) & (c == 0))
    def _():
        run([lower])

    start(new)
    for one in new:
        one.wait()


VMEM = pl.BlockSpec(memory_space=pltpu.VMEM)
ANY = pl.BlockSpec(memory_space=pl.ANY)
PARAMS = pltpu.CompilerParams(vmem_limit_bytes=56 << 20)
TILE = jax.ShapeDtypeStruct((T, T), f32)
PARTS = pltpu.VMEM((T, 3 * T), bf16)
GRID = ("row", "col")


def place(x, y, z, core):
    return (y * 2 + core) * 16 + x * 4 + z


def branches(core, start, order):
    def move(chip, axis, by):
        return tuple((v + by) % 4 if n == axis else v for n, v in enumerate(chip))

    have, rounds = [start], []
    for axis in order:
        new = [move(chip, axis, 1) for chip in have]
        rounds.append(list(zip(have, new)))
        rounds.append(
            [(chip, move(chip, axis, -1)) for chip in have] + [(chip, move(chip, axis, 1)) for chip in new]
        )
        have = have + new + [dst for _, dst in rounds[-1]]
    return [[(place(*src, core), place(*dst, core)) for src, dst in pairs] for pairs in rounds]


def trees():
    first = [
        one + [pair for pair in two if pair[1] != 0]
        for one, two in zip(branches(1, (0, 0, 0), (0, 2, 1)), branches(0, (0, 0, 1), (1, 0, 2)))
    ]
    second = [
        one + two for one, two in zip(branches(1, (0, 1, 0), (0, 2, 1)), branches(0, (0, 1, 0), (1, 0, 2)))
    ]
    chips = [(x, y, z) for x in range(4) for y in range(4) for z in range(4)]
    swap = [(place(*chip, k), place(*chip, 1 - k)) for chip in chips for k in range(2)]
    return first + [swap], second + [swap]


TIE = 9


def wave(curs, late, rows):
    plans = [trees()[k >= late] for k in range(len(curs))]
    curs, count, last = list(curs), len(curs), len(plans[0]) - 1
    pairs, going = [None] * count, {}
    for t in range(count + last + 1):
        arrived, going = going, {}
        for k, got in sorted(arrived.items()):
            after = k + 1 if k >= late else k + 2
            if after < count and (after >= late) == (k >= late):
                got, curs[after] = lax.optimization_barrier((got, curs[after]))
            if t - 1 - k == last:
                pairs[k] = (curs[k], got)
            else:
                curs[k] = curs[k] + got
        if t == TIE:
            rows, curs[-1] = lax.optimization_barrier((rows, curs[-1]))
        for k in range(count):
            if 0 <= t - k <= last:
                going[k] = lax.ppermute(curs[k], GRID, plans[k][t - k])
    return [one for pair in pairs for one in pair], rows


def scatter_rows(tiles):
    flat = tiles[0].reshape(4, T // 4, T)
    shard = None
    for m in range(4):
        pairs = [
            (h * 16 + j, (j % 8) * 16 + (j // 8) * 8 + h * 4 + m)
            for j in range(1, 16)
            for h in range(2)
            if (h, j) != (1, 1)
        ]
        got = lax.ppermute(flat[m], GRID, pairs)
        shard = got if shard is None else shard + got
    return shard


def scatter_cols(tiles):
    flat = tiles[0].reshape(4, T // 4, T)
    shard = None
    for m in range(4):
        pairs = [(h * 16 + c, (h * 4 + m) * 16 + c) for c in range(2, 16) for h in range(2)]
        got = lax.ppermute(flat[m], GRID, pairs)
        shard = got if shard is None else shard + got
    return shard


def cost(us):
    return pl.CostEstimate(flops=int(us * 1e9), bytes_accessed=int(us * 3e6), transcendentals=0)


SHARD = (T // 4, T)
FOLDED = jax.ShapeDtypeStruct((3 * B, T), f32)
WHOLE = pltpu.VMEM((T, T), f32)
SEMS = pltpu.SemaphoreType.DMA((16,))


def kernel_call(body, out_shape, scratch, us, name, count):
    many = isinstance(out_shape, list)
    return pl.pallas_call(
        body,
        out_shape=out_shape,
        in_specs=[ANY] * count,
        out_specs=[ANY] * len(out_shape) if many else ANY,
        scratch_shapes=scratch,
        compiler_params=PARAMS,
        cost_estimate=cost(us),
        name=name,
    )


def shards(kernel):
    tiles = kernel.reshape(2, T, T)
    me = lax.axis_index("row") * 16 + lax.axis_index("col")
    row_shard = scatter_rows(tiles)
    row_shard, tiles = lax.optimization_barrier((row_shard, tiles))
    rows = lax.all_gather(row_shard, "col", axis=0, tiled=True)
    left = lax.ppermute(tiles[0], GRID, [(16, 0)])
    corner = lax.ppermute(tiles[0], GRID, [(17, 0)])
    first, fold0 = pl.pallas_call(
        first_kernel,
        out_shape=[TILE, FOLDED],
        in_specs=[ANY],
        out_specs=[VMEM, VMEM],
        scratch_shapes=[WHOLE, pltpu.SemaphoreType.DMA],
        compiler_params=PARAMS,
        cost_estimate=cost(25),
        name="factor_first",
    )(tiles)
    fold0_one = lax.ppermute(fold0, GRID, [(0, 16)])
    fold0_two = lax.ppermute(fold0, GRID, [(0, 1)])
    fold1 = kernel_call(
        second_kernel, FOLDED, [WHOLE] * 5 + [PARTS, PARTS, SEMS], 30, "factor_second", 3
    )(left, corner, fold0)
    one = lax.ppermute(fold1[:192], GRID, [(0, place(0, 1, 0, 1))])
    two = lax.ppermute(fold1[192:], GRID, [(0, place(0, 1, 0, 0))])
    fold0_one, fold0_two, one, two, tiles = lax.optimization_barrier(
        (fold0_one, fold0_two, one, two, tiles)
    )
    fold0_got = fold0_one + fold0_two
    col_shard = scatter_cols(tiles)
    col_shard, fold0_got, tiles = lax.optimization_barrier((col_shard, fold0_got, tiles))
    cols = lax.all_gather(col_shard, "row", axis=0, tiled=True)
    panel = kernel_call(
        panel_kernel, TILE, [WHOLE] * 3 + [PARTS, PARTS, SEMS], 5, "panel_product", 2
    )(tiles, fold0_got)
    pieces = [fold0_got[p * B : (p + 1) * B] for p in range(3)]
    pieces += [panel[n * B : (n + 1) * B] for n in range(5)]
    curs = [
        jnp.where(me == 16, pieces[2 * k], jnp.where(me == 1, pieces[2 * k + 1], 0.0)) for k in range(4)
    ]
    both = one + two
    moved, rows = wave(curs + [both[:B], both[B:]], 4, rows)
    out = pl.pallas_call(
        last_kernel,
        out_shape=jax.ShapeDtypeStruct((2, T, T), f32),
        in_specs=[ANY] * 18,
        out_specs=ANY,
        scratch_shapes=[pltpu.VMEM((T, 3 * T), f32)] * 2
        + [WHOLE] * 3
        + [pltpu.VMEM((2, T, T), f32)]
        + [pltpu.VMEM((T, WIDE), bf16)] * 2
        + [pltpu.VMEM((2 * T, WIDE), bf16)] * 2
        + [pltpu.VMEM((T, WIDE), f32), pltpu.VMEM((2, T, T), bf16), pltpu.VMEM((T, 2 * T), bf16)]
        + [pltpu.SemaphoreType.DMA((40,))],
        compiler_params=PARAMS,
        cost_estimate=cost(25),
        name="solve_and_update",
    )(tiles, rows, cols, first, fold0, fold0_got, *moved)
    return out.reshape(kernel.shape)


def solution(mesh):
    spec = P(None, "row", None, "col", None, None)
    return jax.shard_map(shards, mesh=mesh, in_specs=(spec,), out_specs=spec, check_vma=False)
```

```python
import functools

import jax
import jax.numpy as jnp
from jax import lax
from jax.experimental import pallas as pl
from jax.experimental.pallas import tpu as pltpu
from jax.sharding import PartitionSpec as P

f32 = jnp.float32
bf16 = jnp.bfloat16
T = 640
B = 128
NB = T // B
SG = 32
HIGHEST = lax.Precision.HIGHEST
NT = (((1,), (1,)), ((), ()))
TN = (((0,), (0,)), ((), ()))


def split3(x):
    high = x.astype(bf16)
    rest = x - high.astype(f32)
    mid = rest.astype(bf16)
    low = (rest - mid.astype(f32)).astype(bf16)
    return high, mid, low


def left6(parts, axis):
    h, m, l = parts
    return jnp.concatenate([h, h, m, m, h, l], axis)


def right6(parts):
    h, m, l = parts
    return jnp.concatenate([h, m, h, m, l, h], 0)


def dot6(left, right):
    return jnp.dot(left, right, preferred_element_type=f32)


def row_of(x, m):
    return jnp.broadcast_to(x[m : m + 1, :], x.shape)


def factor_block(block):
    groups = SG // 8
    row = lax.broadcasted_iota(jnp.int32, (B, B), 0)
    col = lax.broadcasted_iota(jnp.int32, (B, B), 1)
    unit = jnp.where(row == col, 1.0, 0.0)
    sub = lax.broadcasted_iota(jnp.int32, (8, B), 0)
    count = B // SG
    work = [
        jnp.concatenate([block[s * SG : (s + 1) * SG], unit[s * SG : (s + 1) * SG]], 1)
        for s in range(count)
    ]
    uppers, inverses = [], []
    for s in range(count):
        u = [work[s][8 * h : 8 * h + 8, :B] for h in range(groups)]
        w = [work[s][8 * h : 8 * h + 8, B:] for h in range(groups)]
        for g in range(groups):
            base = s * SG + 8 * g
            c = [
                [jnp.broadcast_to(u[h][:, base + m : base + m + 1], (8, B)) for m in range(8)]
                if h >= g
                else None
                for h in range(groups)
            ]
            scale = jnp.zeros((8, B), f32)
            for m in range(8):
                pivot = row_of(c[g][m], m)
                inverse = pltpu.reciprocal(pivot)
                scale = jnp.where(sub == m, lax.rsqrt(pivot), scale)
                u_row = row_of(u[g], m) * inverse
                w_row = row_of(w[g], m) * inverse
                c_row = [row_of(c[g][k], m) * inverse if k > m else None for k in range(8)]
                for h in range(g, groups):
                    factor = c[h][m]
                    if h == g:
                        factor = jnp.where(sub > m, factor, 0.0)
                    for k in range(m + 1, 8):
                        c[h][k] = c[h][k] - factor * c_row[k]
                    u[h] = u[h] - factor * u_row
                    w[h] = w[h] - factor * w_row
            u[g] = u[g] * scale
            w[g] = w[g] * scale
        upper = jnp.concatenate(u, 0)
        inverse = jnp.concatenate(w, 0)
        here = lax.broadcasted_iota(jnp.int32, (SG, B), 0) + s * SG
        upper = jnp.where(lax.broadcasted_iota(jnp.int32, (SG, B), 1) >= here, upper, 0.0)
        uppers.append(upper)
        inverses.append(inverse)
        if s < count - 1:
            left = left6(split3(upper[:, (s + 1) * SG :]), 0)
            right = right6(split3(jnp.concatenate([upper, inverse], 1)))
            change = lax.dot_general(left, right, TN, preferred_element_type=f32)
            for t in range(s + 1, count):
                work[t] = work[t] - change[(t - s - 1) * SG : (t - s) * SG]
    return jnp.concatenate(uppers, 0), jnp.concatenate(inverses, 0)


def factor_tile(read, lower_ref, inverse_ref):
    panel = [read(i) for i in range(NB)]
    aug = [None] * NB
    for i in range(NB):
        for j in range(i + 1, NB):
            lower_ref[i * B : (i + 1) * B, j * B : (j + 1) * B] = jnp.zeros((B, B), f32)
            inverse_ref[i * B : (i + 1) * B, j * B : (j + 1) * B] = jnp.zeros((B, B), f32)
    for b in range(NB):
        upper, inv = factor_block(panel[b][:, :B])
        rows = slice(b * B, (b + 1) * B)
        lower_ref[rows, rows] = upper.T
        inverse_ref[rows, rows] = inv
        left = left6(split3(inv), 1)
        if b > 0:
            w_left = dot6(left, right6(split3(aug[b])))
            inverse_ref[rows, : b * B] = w_left
            w_all = jnp.concatenate([w_left, inv], 1)
        else:
            w_all = inv
        if b == NB - 1:
            break
        w_parts = right6(split3(w_all))
        pieces = [
            dot6(left, right6(split3(panel[b][:, (i - b) * B : (i - b + 1) * B])))
            for i in range(b + 1, NB)
        ]
        u_parts = right6(split3(jnp.concatenate(pieces, 1)))
        for i in range(b + 1, NB):
            off = (i - b) * B
            turned = pieces[i - b - 1].T
            lower_ref[i * B : (i + 1) * B, rows] = turned
            left_i = left6(split3(turned), 1)
            panel[i] = panel[i] - dot6(left_i, u_parts[:, off - B :])
            grown = -dot6(left_i, w_parts)
            if b > 0:
                grown = jnp.concatenate([aug[i] + grown[:, : b * B], grown[:, b * B :]], 1)
            aug[i] = grown


def at_root():
    return (lax.axis_index("row") == 0) & (lax.axis_index("col") == 0)


FOLD = (
    ((512, 128, 640, 0),),
    ((384, 128, 512, 0), (0, 128, 128, 512)),
    ((256, 128, 384, 0), (128, 128, 256, 384)),
)
PLAIN = ((0, 0), (1, 128), (2, 256))


def fold_copies(tile, folded, sems, out, halves=False):
    found = []
    for p, pieces in enumerate(FOLD):
        for row, rows, width, at in pieces:
            if not halves:
                spots = [(row, rows, p * B)]
            elif p < 2:
                spots = [(row, rows, p * 192)]
            else:
                spots = [(row, 64, 128), (row + 64, 64, 320)]
            for first, count, place_at in spots:
                here = tile.at[pl.ds(first, count), pl.ds(0, width)]
                there = folded.at[pl.ds(place_at, count), pl.ds(at, width)]
                src, dst = (here, there) if out else (there, here)
                found.append(pltpu.make_async_copy(src, dst, sems.at[len(found)]))
    return found


def clear_gaps(ref):
    ref[:B, B : 2 * B] = jnp.zeros((B, B), f32)
    ref[2 * B : 3 * B, 3 * B : 4 * B] = jnp.zeros((B, B), f32)


def run(copies):
    for one in copies:
        one.start()
    for one in copies:
        one.wait()


def first_kernel(tiles_ref, lower_ref, fold_ref, inverse, sem):
    @pl.when(at_root())
    def _():
        run([pltpu.make_async_copy(tiles_ref.at[0], lower_ref, sem)])
        blocks = [lower_ref[i * B : (i + 1) * B, i * B :] for i in range(NB)]
        factor_tile(lambda i: blocks[i], lower_ref, inverse)
        for p, pieces in enumerate(FOLD):
            for row, rows, width, at in pieces:
                fold_ref[p * B : (p + 1) * B, at : at + width] = inverse[row : row + rows, :width]


def split2(x):
    high = x.astype(bf16)
    return high, (x - high.astype(f32)).astype(bf16)


def keep_parts(ref, parts):
    for i in range(NB):
        rows = slice(i * B, (i + 1) * B)
        for n, part in enumerate(split3(ref[rows, :])):
            parts[rows, n * T : (n + 1) * T] = part


def stacked(parts, order, rows, depth):
    return jnp.concatenate([parts[rows, n * T : n * T + depth] for n in order], 1)


LEFT = (0, 0, 1, 1, 0, 2)
RIGHT = (0, 1, 0, 1, 2, 0)
GROUPS = ((0, 256, 256), (256, 256, 512), (512, 128, 640))


def times_inverse(tile_ref, inverse_ref, out_ref, tile_parts, inverse_parts):
    keep_parts(tile_ref, tile_parts)
    keep_parts(inverse_ref, inverse_parts)
    for first, count, depth in GROUPS:
        rows = slice(first, first + count)
        left = stacked(tile_parts, LEFT, slice(None), depth)
        right = stacked(inverse_parts, RIGHT, rows, depth)
        out_ref[:, rows] = lax.dot_general(left, right, NT, preferred_element_type=f32)


def second_kernel(
    left_ref, corner_ref, fold_ref, out_ref, left, corner, inverse, panel, lower, parts, more, sems
):
    @pl.when(at_root())
    def _():
        clear_gaps(inverse)
        run(
            fold_copies(inverse, fold_ref, sems, False)
            + [
                pltpu.make_async_copy(left_ref, left, sems.at[14]),
                pltpu.make_async_copy(corner_ref, corner, sems.at[15]),
            ]
        )
        times_inverse(left, inverse, panel, parts, more)
        keep_parts(panel, parts)
        for i in range(NB):
            one = stacked(parts, LEFT, slice(i * B, (i + 1) * B), T)
            two = stacked(parts, RIGHT, slice(i * B, T), T)
            change = lax.dot_general(one, two, NT, preferred_element_type=f32)
            lower[i * B : (i + 1) * B, i * B :] = corner[i * B : (i + 1) * B, i * B :] - change
        blocks = [lower[i * B : (i + 1) * B, i * B :] for i in range(NB)]
        factor_tile(lambda i: blocks[i], lower, inverse)
        run(fold_copies(inverse, out_ref, sems, True, True))


def panel_kernel(tiles_ref, fold_ref, out_ref, tile, inverse, panel, parts, more, sems):
    r = lax.axis_index("row")
    c = lax.axis_index("col")

    @pl.when(r + c == 1)
    def _():
        clear_gaps(inverse)
        run(
            fold_copies(inverse, fold_ref, sems, False)
            + [pltpu.make_async_copy(tiles_ref.at[0], tile, sems.at[15])]
        )

        @pl.when(c == 1)
        def _():
            tile[...] = tile[...].T

        times_inverse(tile, inverse, panel, parts, more)
        run([pltpu.make_async_copy(panel, out_ref, sems.at[15])])


WIDE = 2048
CHUNK = 512


def triangular(w_ref, parts, xh, xl, emit):
    high, low = split2(w_ref[...])
    parts[0] = high
    parts[1] = low

    def step(n, carry):
        at = pl.ds(pl.multiple_of(n * CHUNK, CHUNK), CHUNK)
        for first, count, depth in GROUPS:
            wh = parts[0, first : first + count, :depth]
            wl = parts[1, first : first + count, :depth]
            top = xh[:depth, at]
            both = dot6(jnp.concatenate([wh, wl], 0), top)
            rest = dot6(wh, xl[:depth, at])
            emit(first, count, at, both[:count] + both[count:] + rest)
        return carry

    lax.fori_loop(0, WIDE // CHUNK, step, 0)


def last_kernel(*refs):
    tiles_ref, rows_ref, cols_ref, first_ref, own_ref, got_ref = refs[:6]
    moved = refs[6:18]
    out_ref = refs[18]
    x0, x1, wa, la, wb, tile, xh, xl, yh, yl, yf, parts, lparts, sems = refs[19:]
    r = lax.axis_index("row")
    c = lax.axis_index("col")
    odd = lax.rem(r, 2) == 1
    inner = c > 0
    used = iter(range(40))

    def copy(src, dst, sem=None):
        return pltpu.make_async_copy(src, dst, sems.at[next(used) if sem is None else sem])

    first_x = [
        copy(rows_ref.at[pl.ds(0, T)], x0.at[:, pl.ds(0, T)]),
        copy(rows_ref.at[pl.ds(2 * T, T)], x0.at[:, pl.ds(T, T)]),
        copy(cols_ref.at[pl.ds(0, T)], x0.at[:, pl.ds(2 * T, T)]),
    ]
    second_x = [
        copy(rows_ref.at[pl.ds(T, T)], x1.at[:, pl.ds(0, T)], 30),
        copy(rows_ref.at[pl.ds(3 * T, T)], x1.at[:, pl.ds(T, T)]),
        copy(cols_ref.at[pl.ds(T, T)], x1.at[:, pl.ds(2 * T, T)]),
    ]
    old = [copy(tiles_ref.at[a], tile.at[a]) for a in range(2)]
    new = [copy(tile.at[a], out_ref.at[a]) for a in range(2)]
    lower = copy(first_ref, tile.at[0], next(used))

    def unfold(dst, p, src, ids, part=None):
        found = []
        for row, rows, width, at in FOLD[p]:
            if part is not None:
                row, rows = row + 64 * part, 64
            got = src.at[pl.ds(0, rows), pl.ds(at, width)]
            found.append(copy(got, dst.at[pl.ds(row, rows), pl.ds(0, width)], ids[len(found)]))
        return found

    def take(n):
        return [next(used) for _ in range(n)]

    def both(k):
        cur, swap = moved[2 * k : 2 * k + 2]
        return (swap, cur), (cur, swap)

    def l_copy(n, src, ids):
        return [copy(src, la.at[pl.ds(n * B, B)], ids[0])]

    w0_ids, l_ids, w1_ids = [take(2) for _ in range(3)], [take(1) for _ in range(5)], [take(2) for _ in range(4)]

    def w0_copies(sources):
        return [one for p in range(3) for one in unfold(wa, p, sources[p], w0_ids[p])]

    def w0_case(side):
        return w0_copies([both(0)[side][0], both(0)[side][1], both(1)[side][0]])

    def l_case(side):
        sources = [both(1)[side][1], *both(2)[side], *both(3)[side]]
        return [one for n in range(5) for one in l_copy(n, sources[n], l_ids[n])]

    def w1_case(side):
        pieces, halves = both(4)[side], both(5)[side]
        found = [one for p in range(2) for one in unfold(wb, p, pieces[p], w1_ids[p])]
        return found + [one for h in range(2) for one in unfold(wb, 2, halves[h], w1_ids[2 + h], h)]

    def whole(ref):
        return w0_copies([ref.at[pl.ds(p * B, B)] for p in range(3)])

    def start(copies):
        for one in copies:
            one.start()

    def wait(copies):
        for one in copies:
            one.wait()

    for one in first_x:
        one.start()

    clear_gaps(wa)

    @pl.when((c == 0) & (r == 0))
    def _():
        start(whole(own_ref))

    @pl.when((c == 0) & (r == 1))
    def _():
        start(whole(got_ref))

    far = (c > 0) | (r > 1)
    for side in range(2):

        @pl.when(far & (odd if side else jnp.logical_not(odd)))
        def _():
            start(w0_case(side))

    @pl.when((r == 1) & (c == 1))
    def _():
        copy(tiles_ref.at[0], x1.at[:, pl.ds(0, T)], 30).start()

    @pl.when(inner & ((r != 1) | (c != 1)))
    def _():
        second_x[0].start()

    @pl.when(inner)
    def _():
        start(second_x[1:])
        clear_gaps(wb)
        start(old)

    for side in range(2):

        @pl.when(inner & (odd if side else jnp.logical_not(odd)))
        def _():
            start(l_case(side))
            start(w1_case(side))

    for one in first_x:
        one.wait()

    def cut(i, carry):
        rows = pl.ds(pl.multiple_of(i * B, B), B)
        xh[rows, : 3 * T], xl[rows, : 3 * T] = split2(x0[rows, :])
        return carry

    lax.fori_loop(0, NB, cut, 0)

    wait(w0_case(0))

    def emit(base):
        def store(first, count, at, y):
            rows = slice(base + first, base + first + count)
            yh[rows, at], yl[rows, at] = split2(y)
            yf[first : first + count, at] = y

        return store

    triangular(wa, parts, xh, xl, emit(0))

    @pl.when(inner)
    def _():
        for one in second_x:
            one.wait()
        wait(l_case(0))
        lparts[:, :T], lparts[:, T:] = split2(la[...])

        def step(i, carry):
            at = pl.ds(pl.multiple_of(i * T, B), T)
            left = jnp.concatenate([lparts[:, :T], lparts[:, :T], lparts[:, T:]], 1)
            high = yh[:T, at]
            right = jnp.concatenate([high, yl[:T, at], high], 0)
            xh[:, at], xl[:, at] = split2(x1[:, at] - dot6(left, right))
            return carry

        lax.fori_loop(0, 3, step, 0)
        wait(w1_case(0))
        triangular(wb, parts, xh, xl, emit(T))
        for one in old:
            one.wait()

    @pl.when(r == 1)
    def _():
        yh[T:, :T] = jnp.zeros((T, T), bf16)
        yl[T:, :T] = jnp.zeros((T, T), bf16)

    def update(n, carry):
        a = n // NB
        top = r + 8 * a

        @pl.when((c > 1) & (top > 0))
        def _():
            at = pl.ds(pl.multiple_of(n * B, B), B)
            rows = pl.ds(pl.multiple_of((n - a * NB) * B, B), B)
            high = yh[:, at]
            left = jnp.concatenate([high, yl[:, at]], 1)
            both = lax.dot_general(left, yh[:, 2 * T : 3 * T], TN, preferred_element_type=f32)
            rest = lax.dot_general(high, yl[:, 2 * T : 3 * T], TN, preferred_element_type=f32)
            tile[a, rows, :] = tile[a, rows, :] - (both[:B] + both[B:] + rest)

        @pl.when((top > 0) & (c < 2))
        def _():
            at = pl.ds(pl.multiple_of(n * B, B), B)
            rows = pl.ds(pl.multiple_of((n - a * NB) * B, B), B)
            row = lax.broadcasted_iota(jnp.int32, (B, T), 0) + (n - a * NB) * B
            col = lax.broadcasted_iota(jnp.int32, (B, T), 1)
            tile[a, rows, :] = jnp.where((top == 1) & (c == 1) & (col > row), 0.0, yf[:, at].T)

        return carry

    lax.fori_loop(0, 2 * NB, update, 0)

    @pl.when((r == 0) & (c == 0))
    def _():
        run([lower])

    start(new)
    for one in new:
        one.wait()


VMEM = pl.BlockSpec(memory_space=pltpu.VMEM)
ANY = pl.BlockSpec(memory_space=pl.ANY)
PARAMS = pltpu.CompilerParams(vmem_limit_bytes=56 << 20)
TILE = jax.ShapeDtypeStruct((T, T), f32)
PARTS = pltpu.VMEM((T, 3 * T), bf16)
GRID = ("row", "col")


def place(x, y, z, core):
    return (y * 2 + core) * 16 + x * 4 + z


def branches(core, start, order):
    def move(chip, axis, by):
        return tuple((v + by) % 4 if n == axis else v for n, v in enumerate(chip))

    have, rounds = [start], []
    for axis in order:
        new = [move(chip, axis, 1) for chip in have]
        rounds.append(list(zip(have, new)))
        rounds.append(
            [(chip, move(chip, axis, -1)) for chip in have] + [(chip, move(chip, axis, 1)) for chip in new]
        )
        have = have + new + [dst for _, dst in rounds[-1]]
    return [[(place(*src, core), place(*dst, core)) for src, dst in pairs] for pairs in rounds]


def trees():
    first = [
        one + [pair for pair in two if pair[1] != 0]
        for one, two in zip(branches(1, (0, 0, 0), (0, 2, 1)), branches(0, (0, 0, 1), (1, 0, 2)))
    ]
    second = [
        one + two for one, two in zip(branches(1, (0, 1, 0), (0, 2, 1)), branches(0, (0, 1, 0), (1, 0, 2)))
    ]
    chips = [(x, y, z) for x in range(4) for y in range(4) for z in range(4)]
    swap = [(place(*chip, k), place(*chip, 1 - k)) for chip in chips for k in range(2)]
    return first + [swap], second + [swap]


TIE = 9


def wave(curs, late, rows, cols):
    plans = [trees()[k >= late] for k in range(len(curs))]
    curs, count, last = list(curs), len(curs), len(plans[0]) - 1
    pairs, going = [None] * count, {}
    for t in range(count + last + 1):
        arrived, going = going, {}
        for k, got in sorted(arrived.items()):
            after = k + 1 if k >= late else k + 2
            if after < count and (after >= late) == (k >= late):
                got, curs[after] = lax.optimization_barrier((got, curs[after]))
            if t - 1 - k == last:
                pairs[k] = (curs[k], got)
            else:
                curs[k] = curs[k] + got
        if t == TIE:
            rows, cols, curs[-1] = lax.optimization_barrier((rows, cols, curs[-1]))
        for k in range(count):
            if 0 <= t - k <= last:
                going[k] = lax.ppermute(curs[k], GRID, plans[k][t - k])
    return [one for pair in pairs for one in pair], rows, cols


def scatter_rows(tiles):
    flat = tiles[0].reshape(4, T // 4, T)
    shard = None
    for m in range(4):
        pairs = [
            (h * 16 + j, (j % 8) * 16 + (j // 8) * 8 + h * 4 + m)
            for j in range(1, 16)
            for h in range(2)
            if (h, j) != (1, 1)
        ]
        got = lax.ppermute(flat[m], GRID, pairs)
        shard = got if shard is None else shard + got
    return shard


def cost(us):
    return pl.CostEstimate(flops=int(us * 1e9), bytes_accessed=int(us * 3e6), transcendentals=0)


SHARD = (T // 4, T)
FOLDED = jax.ShapeDtypeStruct((3 * B, T), f32)
WHOLE = pltpu.VMEM((T, T), f32)
SEMS = pltpu.SemaphoreType.DMA((16,))


def kernel_call(body, out_shape, scratch, us, name, count):
    many = isinstance(out_shape, list)
    return pl.pallas_call(
        body,
        out_shape=out_shape,
        in_specs=[ANY] * count,
        out_specs=[ANY] * len(out_shape) if many else ANY,
        scratch_shapes=scratch,
        compiler_params=PARAMS,
        cost_estimate=cost(us),
        name=name,
    )


def shards(kernel):
    tiles = kernel.reshape(2, T, T)
    me = lax.axis_index("row") * 16 + lax.axis_index("col")
    r = me // 16
    top, none = tiles[0], jnp.zeros((T, T), f32)
    cols = lax.psum(
        jnp.concatenate([jnp.where(r == 0, top, none), jnp.where(r == 1, top, none)], 0), "row"
    )
    row_shard = scatter_rows(tiles)
    row_shard, tiles = lax.optimization_barrier((row_shard, tiles))
    rows = lax.all_gather(row_shard, "col", axis=0, tiled=True)
    left = lax.ppermute(tiles[0], GRID, [(16, 0)])
    corner = lax.ppermute(tiles[0], GRID, [(17, 0)])
    first, fold0 = pl.pallas_call(
        first_kernel,
        out_shape=[TILE, FOLDED],
        in_specs=[ANY],
        out_specs=[VMEM, VMEM],
        scratch_shapes=[WHOLE, pltpu.SemaphoreType.DMA],
        compiler_params=PARAMS,
        cost_estimate=cost(25),
        name="factor_first",
    )(tiles)
    fold0_one = lax.ppermute(fold0, GRID, [(0, 16)])
    fold0_two = lax.ppermute(fold0, GRID, [(0, 1)])
    fold1 = kernel_call(
        second_kernel, FOLDED, [WHOLE] * 5 + [PARTS, PARTS, SEMS], 30, "factor_second", 3
    )(left, corner, fold0)
    one = lax.ppermute(fold1[:192], GRID, [(0, place(0, 1, 0, 1))])
    two = lax.ppermute(fold1[192:], GRID, [(0, place(0, 1, 0, 0))])
    fold0_one, fold0_two, one, two, tiles = lax.optimization_barrier(
        (fold0_one, fold0_two, one, two, tiles)
    )
    fold0_got = fold0_one + fold0_two
    tiles, fold0_got = lax.optimization_barrier((tiles, fold0_got))
    panel = kernel_call(
        panel_kernel, TILE, [WHOLE] * 3 + [PARTS, PARTS, SEMS], 5, "panel_product", 2
    )(tiles, fold0_got)
    pieces = [fold0_got[p * B : (p + 1) * B] for p in range(3)]
    pieces += [panel[n * B : (n + 1) * B] for n in range(5)]
    curs = [
        jnp.where(me == 16, pieces[2 * k], jnp.where(me == 1, pieces[2 * k + 1], 0.0)) for k in range(4)
    ]
    both = one + two
    moved, rows, cols = wave(curs + [both[:B], both[B:]], 4, rows, cols)
    out = pl.pallas_call(
        last_kernel,
        out_shape=jax.ShapeDtypeStruct((2, T, T), f32),
        in_specs=[ANY] * 18,
        out_specs=ANY,
        scratch_shapes=[pltpu.VMEM((T, 3 * T), f32)] * 2
        + [WHOLE] * 3
        + [pltpu.VMEM((2, T, T), f32)]
        + [pltpu.VMEM((T, WIDE), bf16)] * 2
        + [pltpu.VMEM((2 * T, WIDE), bf16)] * 2
        + [pltpu.VMEM((T, WIDE), f32), pltpu.VMEM((2, T, T), bf16), pltpu.VMEM((T, 2 * T), bf16)]
        + [pltpu.SemaphoreType.DMA((40,))],
        compiler_params=PARAMS,
        cost_estimate=cost(25),
        name="solve_and_update",
    )(tiles, rows, cols, first, fold0, fold0_got, *moved)
    return out.reshape(kernel.shape)


def solution(mesh):
    spec = P(None, "row", None, "col", None, None)
    return jax.shard_map(shards, mesh=mesh, in_specs=(spec,), out_specs=spec, check_vma=False)
```
